128 devices in a mesh: prow: 8 (over z, core), pcol: 8 (over y_hi, x), orb: 2 (over y_lo).
Axes of the slice: x: 4, y: 4 (y_hi: 2, y_lo: 2; y = y_hi * 2 + y_lo), z: 4, core: 2. Of those that a mesh axis runs over, the one named last changes fastest.
Arguments:
- g2_re: float32 [4096, 4096], P('prow', ('pcol', 'orb')), may hold values from -1 to 1
- g2_im: float32 [4096, 4096], P('prow', ('pcol', 'orb')), may hold values from -1 to 1
- g1_re: float32 [64, 64], P('prow', ('pcol', 'orb')), may hold values from -3 to 3
- g1_im: float32 [64, 64], P('prow', ('pcol', 'orb')), may hold values from -3 to 3
- hop_re: float32 [64, 64], replicated, may hold values from -0.75 to 0.75
- hop_im: float32 [64, 64], replicated, may hold values from -0.75 to 0.75
- coupling: float32 [64, 64], replicated, may hold values from 0.2 to 1.5
Outputs:
- dg2_re: float32 [4096, 4096], P('prow', ('pcol', 'orb'))
- dg2_im: float32 [4096, 4096], P('prow', ('pcol', 'orb'))
- dg1_re: float32 [64, 64], replicated
- dg1_im: float32 [64, 64], replicated
The draws below stay inside these ranges and needn't reach their ends.
All inputs are finite; a program needn't handle non-finite values.
Results may differ from the reference program's by a relative error of at most 0.000076.
Values sent between devices are 32-bit elements; how exact they have to be, the bound alone decides.
A program may use at most 192 MiB of HBM per device.

```python
import jax
import jax.numpy as jnp
from jax import lax

ORBITALS = 64
PAIRS = 4096


def block_scale(key, extent, shards, least, high):
    gain = 1.0
    for dim, shards_of in shards:
        steps = jax.random.uniform(jax.random.fold_in(jax.random.fold_in(key, 6), dim), (shards_of,), jnp.float32, least / len(shards), high / len(shards))
        gain = gain * jnp.repeat(jnp.exp(steps), extent[dim] // shards_of).reshape((-1,) + (1,) * (len(extent) - 1 - dim))
    return gain


def centred(rng, dims, scale, reach, shards=(), held_as=jnp.bfloat16):
    array = jax.random.normal(rng, dims, jnp.float32) * scale
    if len(shards) > 0:
        array = block_scale(rng, dims, shards, -0.22, 0.18) * array
    return jnp.clip(array, min=-reach, max=reach).astype(held_as)


def setup_inputs(seed: int = 0) -> dict:
    splits = jax.random.split(jax.random.key(seed), 8)
    g2_re = centred(splits[0], (PAIRS, PAIRS), 0.125, 1.0, ((0, 8), (1, 16)), jnp.float32)
    g2_im = centred(splits[1], (PAIRS, PAIRS), 0.125, 1.0, ((0, 8), (1, 16)), jnp.float32)
    g1_re = centred(splits[2], (ORBITALS, ORBITALS), 0.5, 3.0, ((0, 8), (1, 16)), jnp.float32)
    g1_im = centred(splits[3], (ORBITALS, ORBITALS), 0.5, 3.0, ((0, 8), (1, 16)), jnp.float32)
    hop_re = centred(splits[4], (ORBITALS, ORBITALS), ORBITALS ** -0.5, 0.75, (), jnp.float32)
    hop_im = centred(splits[5], (ORBITALS, ORBITALS), ORBITALS ** -0.5, 0.75, (), jnp.float32)
    coupling = jnp.clip(jax.random.uniform(splits[6], (ORBITALS, ORBITALS), jnp.float32, 0.2, 1.5), 0.2, 1.5)
    return {"g2_re": g2_re, "g2_im": g2_im, "g1_re": g1_re, "g1_im": g1_im, "hop_re": hop_re, "hop_im": hop_im, "coupling": coupling}


HIGH = lax.Precision.HIGHEST


def hermitian(hop_re, hop_im):
    return 0.5 * (hop_re + hop_re.T), 0.5 * (hop_im - hop_im.T)


def contract(form, left_re, left_im, right_re, right_im):
    real_part = jnp.einsum(form, left_re, right_re, precision=HIGH) - jnp.einsum(form, left_im, right_im, precision=HIGH)
    imag_part = jnp.einsum(form, left_re, right_im, precision=HIGH) + jnp.einsum(form, left_im, right_re, precision=HIGH)
    return real_part, imag_part


def reference(g2_re, g2_im, g1_re, g1_im, hop_re, hop_im, coupling):
    orbits = ORBITALS
    pairs = PAIRS
    field_re, field_im = hermitian(hop_re, hop_im)
    density = jnp.diagonal(g1_re)
    hartree = jnp.dot(coupling, density, precision=HIGH)
    field_re = field_re + jnp.diag(hartree)
    tensor_re = g2_re.reshape(orbits, orbits, orbits, orbits)
    tensor_im = g2_im.reshape(orbits, orbits, orbits, orbits)
    hole_re = tensor_re.transpose(0, 3, 2, 1).reshape(pairs, pairs)
    hole_im = tensor_im.transpose(0, 3, 2, 1).reshape(pairs, pairs)
    weights = coupling.reshape(pairs, 1)
    scaled_re = weights * hole_re
    scaled_im = weights * hole_im
    polar_re = jnp.dot(hole_re, scaled_re, precision=HIGH) - jnp.dot(hole_im, scaled_im, precision=HIGH)
    polar_im = jnp.dot(hole_re, scaled_im, precision=HIGH) + jnp.dot(hole_im, scaled_re, precision=HIGH)
    polar_re = polar_re.reshape(orbits, orbits, orbits, orbits).transpose(0, 3, 2, 1)
    polar_im = polar_im.reshape(orbits, orbits, orbits, orbits).transpose(0, 3, 2, 1)
    major_left = contract('ip,pjkl->ijkl', field_re, field_im, tensor_re, tensor_im)
    minor_left = contract('jp,ipkl->ijkl', field_re, field_im, tensor_re, tensor_im)
    major_right = contract('ijql,qk->ijkl', tensor_re, tensor_im, field_re, field_im)
    minor_right = contract('ijkq,ql->ijkl', tensor_re, tensor_im, field_re, field_im)
    spread = coupling[:, :, None, None] - coupling[None, None, :, :]
    total_re = polar_re + major_left[0] + minor_left[0] - major_right[0] - minor_right[0] + spread * tensor_re
    total_im = polar_im + major_left[1] + minor_left[1] - major_right[1] - minor_right[1] + spread * tensor_im
    dg2_re = total_im.reshape(pairs, pairs)
    dg2_im = -total_re.reshape(pairs, pairs)
    diagonal_re = jnp.diagonal(tensor_re, axis1=1, axis2=3)
    diagonal_im = jnp.diagonal(tensor_im, axis1=1, axis2=3)
    source_re = jnp.einsum('ijk,ik->ij', diagonal_re, coupling, precision=HIGH)
    source_im = jnp.einsum('ijk,ik->ij', diagonal_im, coupling, precision=HIGH)
    collide_re = source_im
    collide_im = -source_re
    left_re = jnp.dot(field_re, g1_re, precision=HIGH) - jnp.dot(field_im, g1_im, precision=HIGH)
    left_im = jnp.dot(field_re, g1_im, precision=HIGH) + jnp.dot(field_im, g1_re, precision=HIGH)
    right_re = jnp.dot(g1_re, field_re, precision=HIGH) - jnp.dot(g1_im, field_im, precision=HIGH)
    right_im = jnp.dot(g1_re, field_im, precision=HIGH) + jnp.dot(g1_im, field_re, precision=HIGH)
    commute_re = left_re - right_re
    commute_im = left_im - right_im
    dg1_re = commute_im + collide_re + collide_re.T
    dg1_im = -commute_re + collide_im - collide_im.T
    return dg2_re, dg2_im, dg1_re, dg1_im
```

```python
import functools

import jax
import jax.numpy as jnp
from jax import lax
from jax.experimental import pallas as pl
from jax.experimental.pallas import tpu as pltpu
from jax.sharding import PartitionSpec as P

HIGH = lax.Precision.HIGHEST
MESH = pl.DeviceIdType.MESH
F32 = jnp.float32
BF16 = jnp.bfloat16

ORB = 64
ROWS = 8
COLS = 4


def dot(a, b):
    return jnp.dot(a, b, precision=HIGH, preferred_element_type=F32)


def mxu(a, b):
    return jnp.dot(a, b, preferred_element_type=F32)


def iota(shape, dim):
    return lax.broadcasted_iota(jnp.int32, shape, dim)


def split(value):
    high = value.astype(BF16)
    return high, (value - high.astype(F32)).astype(BF16)


def half_swap(first, second, lower):
    return (
        jnp.where(lower, first, pltpu.roll(second, 64, 1)),
        jnp.where(lower, pltpu.roll(first, 64, 1), second),
    )


def kernel(
    g2r,
    g2i,
    g1r,
    g1i,
    hop_r,
    hop_i,
    coup,
    hop_r_s,
    hop_i_s,
    out_r,
    out_i,
    d1_r,
    d1_i,
    right,
    left,
    left_send,
    stack,
    lcat,
    part,
    part_in,
    small_y,
    small_x,
    small_z,
    field_rows,
    kron,
    wide,
    send,
    recv,
):
    prow, pcol, orb = (lax.axis_index(n) for n in ("prow", "pcol", "orb"))
    z, c = prow // 2, prow % 2
    x = pcol % 4
    y = (pcol // 4) * 2 + orb
    rb = prow

    def at(dx=0, dy=0, dz=0, dc=0):
        xx, yy, zz, cc = (x + dx) % 4, (y + dy) % 4, (z + dz) % 4, (c + dc) % 2
        return (zz * 2 + cc, (yy // 2) * 4 + xx, yy % 2)

    def col_block(xx, yy):
        return (yy // 2) * 8 + xx * 2 + yy % 2

    cb = col_block(x, y)
    ya = y + 1 - 2 * orb
    yb = (y + 3 + 2 * orb) % 4
    dev_a = (prow, (ya // 2) * 4 + x, ya % 2)
    dev_b = (prow, (yb // 2) * 4 + x, yb % 2)

    partners = [
        at(dc=1),
        at(dx=1),
        at(dx=3),
        at(dx=2),
        at(dy=1),
        at(dy=3),
        at(dy=2),
        at(dz=1),
        at(dz=3),
        at(dz=2),
    ]
    barrier = pltpu.get_barrier_semaphore()
    for device in partners:
        pl.semaphore_signal(barrier, inc=1, device_id=device, device_id_type=MESH)

    sent = []

    def push(src, dst, device):
        n = len(sent)
        copy = pltpu.make_async_remote_copy(
            src_ref=src,
            dst_ref=dst,
            send_sem=send.at[n],
            recv_sem=recv.at[n],
            device_id=device,
            device_id_type=MESH,
        )
        copy.start()
        sent.append(copy)
        return copy

    lower = iota((64, 128), 1) < 64
    for comp, g in ((0, g2r), (1, g2i)):
        for kt in range(2):
            lanes = slice(kt * 128, kt * 128 + 128)
            for ip in range(4):
                even, odd = half_swap(
                    g[ip * 128 : ip * 128 + 64, lanes],
                    g[ip * 128 + 64 : ip * 128 + 128, lanes],
                    lower,
                )
                to = slice(ip * 128, ip * 128 + 128)
                right[0, 2 * kt, comp, :, to] = even
                right[0, 2 * kt + 1, comp, :, to] = odd
    mine = pl.ds(pl.multiple_of(orb * 256, 256), 256)
    other = pl.ds(pl.multiple_of((1 - orb) * 256, 256), 256)
    for comp in range(2):
        for k in range(4):
            left[rb, 0, comp, k * 64 : k * 64 + 64, :] = right[0, k, comp, :, mine]
            left_send[k // 2, comp, (k % 2) * 64 : (k % 2) * 64 + 64, :] = right[
                0, k, comp, :, other
            ]

    same = iota((64, 256), 0) == iota((64, 256), 1) % 64
    repeat = same.astype(F32)
    wide[...] = dot(coup[...], repeat)
    diag_r = jnp.concatenate(
        [jnp.sum(jnp.where(same, g2r[i * 64 : i * 64 + 64, :], 0.0), 0, keepdims=True) for i in range(ROWS)], 0
    )
    diag_i = jnp.concatenate(
        [jnp.sum(jnp.where(same, g2i[i * 64 : i * 64 + 64, :], 0.0), 0, keepdims=True) for i in range(ROWS)], 0
    )
    weight = wide[pl.ds(pl.multiple_of(rb * ROWS, ROWS), ROWS), :]
    place = iota((256, 128), 1) - COLS * cb
    group = iota((256, 128), 0) // 64
    to_re = (place == group).astype(F32)
    to_im = (place == group + 64).astype(F32)
    small_y[0, 8:16, :] = dot(weight * diag_i, to_re) - dot(weight * diag_r, to_im)
    spot = iota((8, 128), 1) - COLS * cb
    tile = jnp.zeros((8, 128), F32)
    for q in range(COLS):
        tile = tile + jnp.where(spot == q, g1r[:, q : q + 1], 0.0)
        tile = tile + jnp.where(spot == q + 64, g1i[:, q : q + 1], 0.0)
    small_y[0, 0:8, :] = tile

    pl.semaphore_wait(barrier, len(partners))

    tiny_y = [
        push(small_y.at[0], small_y.at[n], at(dy=d)) for n, d in ((1, 1), (2, 3), (3, 2))
    ]
    pre = [
        push(left_send.at[0], left.at[rb, 1, :, 0:128, :], dev_a),
        push(left_send.at[1], left.at[rb, 1, :, 128:256, :], dev_b),
    ]
    z_first = {}
    for d, name in ((1, "m"), (3, "p")):
        z_first[name, 0] = push(left.at[rb, 0], left.at[rb, 0], at(dz=d))
    got = {}
    for a in range(4):
        got[1, a] = push(right.at[0, a], right.at[1, a], at(dy=2))
        got[2, a] = push(right.at[0, a], right.at[2, a], at(dx=1))
        got[4, a] = push(right.at[0, a], right.at[4, a], at(dx=3))
    sib = [push(left.at[rb, 0], left.at[rb, 0], at(dc=1))]

    eye = (iota((64, 64), 0) == iota((64, 64), 1)).astype(F32)
    hr, hi = hop_r[...], hop_i[...]
    off_r = 0.5 * (hr + hr.T) * (1.0 - eye)
    off_i = 0.5 * (hi - hi.T)
    choose = (iota((64, 512), 0) == rb * ROWS + iota((64, 512), 1) // 64).astype(F32)
    field_rows[0] = dot(off_r, choose)
    field_rows[1] = -dot(off_i, choose)
    block_diag = iota((256, 256), 0) // 64 == iota((256, 256), 1) // 64
    tall = (iota((256, 64), 0) % 64 == iota((256, 64), 1)).astype(F32)
    kron[0] = jnp.where(block_diag, dot(tall, dot(off_r, repeat)), 0.0)
    kron[1] = jnp.where(block_diag, dot(tall, dot(off_i, repeat)), 0.0)
    coup_t = coup[...].T

    def where_is(slot):
        dx = (0, 3, 1, 2)[slot // 2]
        return (x + dx) % 4, (y + 2 * (slot % 2)) % 4

    def prepare(slot):
        base = col_block(*where_is(slot)) * COLS
        match = iota((64, 512), 0) == iota((64, 512), 1) % 64
        for a in range(4):
            v = jnp.sum(
                jnp.where(iota((64, 64), 1) == base + a, coup_t, 0.0), 1, keepdims=True
            )
            for comp in range(2):
                value = v * right[slot, a, comp] + jnp.where(
                    match, field_rows[comp, pl.ds(base + a, 1), :], 0.0
                )
                high, low = split(value)
                at_row = comp * 256 + a * 64
                stack[slot, at_row : at_row + 64, :] = high
                stack[slot, 512 + at_row : 512 + at_row + 64, :] = low

    def mix(slot):
        base = col_block(*where_is(slot)) * COLS
        starts = (cb * COLS, col_block(x, ya) * COLS, col_block(x, yb) * COLS)
        scale = {}
        for kk in range(8):
            k = starts[0] + kk if kk < 4 else starts[1 if kk < 6 else 2] + kk - 4
            for a in range(4):
                if slot == 0 and a == kk:
                    continue
                scale[kk, a] = (
                    0.5 * (hop_r_s[base + a, k] + hop_r_s[k, base + a]),
                    0.5 * (hop_i_s[base + a, k] - hop_i_s[k, base + a]),
                )

        @pl.loop(0, 16)
        def _(step):
            strip, half = step // 2, step % 2
            lanes = pl.ds(pl.multiple_of(half * 256, 256), 256)
            rows = pl.ds(pl.multiple_of(strip * 8, 8), 8)
            tr = [right[slot, a, 0, rows, lanes] for a in range(4)]
            ti = [right[slot, a, 1, rows, lanes] for a in range(4)]
            for kk in range(8):
                to = pl.ds(pl.multiple_of((kk % 2) * 64 + strip * 8, 8), 8)
                acc_r = acc_i = None
                for a in range(4):
                    if (kk, a) not in scale:
                        continue
                    sr, si = scale[kk, a]
                    vr = si * ti[a] - sr * tr[a]
                    vi = sr * ti[a] + si * tr[a]
                    acc_r = vr if acc_r is None else acc_r + vr
                    acc_i = -vi if acc_i is None else acc_i - vi
                if slot == 0:
                    part[kk // 2, 0, to, lanes] = acc_r
                    part[kk // 2, 1, to, lanes] = acc_i
                else:
                    part[kk // 2, 0, to, lanes] += acc_r
                    part[kk // 2, 1, to, lanes] += acc_i

    def multiply(slot, half):
        xx, yy = where_is(slot)
        which = (yy // 2) * 4 + xx
        lr_h, lr_l = split(left[which, half, 0])
        li_h, li_l = split(left[which, half, 1])
        for n, (re, im) in enumerate(((lr_h, li_h), (lr_l, li_l))):
            lcat[0, :, n * 512 : n * 512 + 256] = re
            lcat[0, :, n * 512 + 256 : n * 512 + 512] = -im
            lcat[1, :, n * 512 : n * 512 + 256] = im
            lcat[1, :, n * 512 + 256 : n * 512 + 512] = re

        @pl.loop(0, 4)
        def _(step):
            comp, side = step // 2, step % 2
            lanes = pl.ds(pl.multiple_of(side * 256, 256), 256)
            high = lcat[comp, :, 0:512]
            value = (
                mxu(high, stack[slot, 0:512, lanes])
                + mxu(high, stack[slot, 512:1024, lanes])
                + mxu(lcat[comp, :, 512:1024], stack[slot, 0:512, lanes])
            )
            part[2 * half, comp, :, lanes] += value[0:128]
            part[2 * half + 1, comp, :, lanes] += value[128:256]

    prepare(0)
    mix(0)

    for copy in tiny_y:
        copy.wait_recv()
    small_x[0] = small_y[0] + small_y[1] + small_y[2] + small_y[3]
    tiny_x = [
        push(small_x.at[0], small_x.at[n], at(dx=d)) for n, d in ((1, 1), (2, 3), (3, 2))
    ]

    for copy in pre:
        copy.wait_recv()
    for d, name in ((1, "m"), (3, "p")):
        z_first[name, 1] = push(left.at[rb, 1], left.at[rb, 1], at(dz=d))
    sib.append(push(left.at[rb, 1], left.at[rb, 1], at(dc=1)))

    for half in range(2):
        rows = slice(half * 256, half * 256 + 256)
        gr, gi = g2r[rows, :], g2i[rows, :]
        kr, ki = kron[0], kron[1]
        out_r[rows, :] = dot(kr, gi) + dot(ki, gr) - dot(gr, ki) - dot(gi, kr)
        out_i[rows, :] = dot(ki, gi) - dot(kr, gr) + dot(gr, kr) - dot(gi, ki)

    for copy in tiny_x:
        copy.wait_recv()
    small_z[c, z] = small_x[0] + small_x[1] + small_x[2] + small_x[3]
    tiny_z = [
        push(small_z.at[c, z], small_z.at[c, z], at(dz=d)) for d in (1, 3, 2)
    ]

    rb_m = ((z + 3) % 4) * 2 + c
    rb_p = ((z + 1) % 4) * 2 + c
    rb_2 = ((z + 2) % 4) * 2 + c
    z_second = {}

    def pass_on(p):
        z_first["m", p].wait_recv()
        z_second[0, p] = push(left.at[rb_m, p, 0], left.at[rb_m, p, 0], at(dz=1))
        sib.append(push(left.at[rb_m, p], left.at[rb_m, p], at(dc=1)))
        z_first["p", p].wait_recv()
        z_second[1, p] = push(left.at[rb_p, p, 1], left.at[rb_p, p, 1], at(dz=3))
        sib.append(push(left.at[rb_p, p], left.at[rb_p, p], at(dc=1)))

    pass_on(0)

    for copy in tiny_z:
        copy.wait_recv()
    tiny_c = push(small_z.at[c], small_z.at[c], at(dc=1))

    for a in range(3):
        got[1, a].wait_recv()
        got[3, a] = push(right.at[1, a], right.at[3, a], at(dx=1))
        got[5, a] = push(right.at[1, a], right.at[5, a], at(dx=3))
    got[1, 3].wait_recv()
    prepare(1)
    mix(1)
    tiny_c.wait_recv()

    rows_z = [(r // 2, r % 2) for r in range(8)]
    one = jnp.concatenate([small_z[cc, zz, 0:8, :] for zz, cc in rows_z], 0)
    coll = jnp.concatenate([small_z[cc, zz, 8:16, :] for zz, cc in rows_z], 0)
    gr, gi = one[:, 0:64], one[:, 64:128]
    cr, ci = coll[:, 0:64], coll[:, 64:128]
    density = jnp.sum(gr * eye, 0, keepdims=True)
    hartree_col = jnp.sum(coup[...] * density, 1, keepdims=True)
    diag_col = hartree_col + jnp.sum(hr * eye, 1, keepdims=True)
    diag_row = jnp.sum(diag_col * eye, 0, keepdims=True)
    fr = off_r + diag_col * eye
    fi = off_i
    comm_r = dot(fr, gr) - dot(fi, gi) - dot(gr, fr) + dot(gi, fi)
    comm_i = dot(fr, gi) + dot(fi, gr) - dot(gr, fi) - dot(gi, fr)
    d1_r[...] = comm_i + cr + cr.T
    d1_i[...] = ci - ci.T - comm_r

    from_cols = jnp.zeros((1, 256), F32)
    lane_group = iota((1, 256), 1) // 64
    row64 = iota((64, 64), 0)
    table = coup[...] + diag_col + diag_row
    table_wide = dot(table, repeat)
    row_wide = iota((64, 256), 0)
    for k in range(COLS):
        picked = jnp.sum(
            jnp.where(row_wide == cb * COLS + k, table_wide, 0.0), 0, keepdims=True
        )
        from_cols = jnp.where(lane_group == k, picked, from_cols)
    table_t = coup_t + diag_col + diag_row
    for i in range(ROWS):
        from_rows = jnp.sum(
            jnp.where(iota((64, 64), 1) == rb * ROWS + i, table_t, 0.0), 1, keepdims=True
        )
        rows = slice(i * 64, i * 64 + 64)
        factor = from_rows - from_cols
        out_r[rows, :] += factor * g2i[rows, :]
        out_i[rows, :] -= factor * g2r[rows, :]

    for a in range(4):
        got[2, a].wait_recv()
        got[4, a].wait_recv()
        if a < 3:
            got[6, a] = push(right.at[2, a], right.at[6, a], at(dx=1))
        else:
            last = [
                push(right.at[2, 3, 0], right.at[6, 3, 0], at(dx=1)),
                push(right.at[4, 3, 1], right.at[6, 3, 1], at(dx=3)),
            ]
            got[3, 3] = push(right.at[2, 3], right.at[3, 3], at(dy=2))
            got[5, 3] = push(right.at[4, 3], right.at[5, 3], at(dy=2))
    pass_on(1)
    prepare(2)
    mix(2)
    prepare(4)
    mix(4)
    z_second[0, 0].wait_recv()
    z_second[1, 0].wait_recv()
    sib.append(push(left.at[rb_2, 0], left.at[rb_2, 0], at(dc=1)))
    for copy in last:
        copy.wait_recv()
    got[7, 3] = push(right.at[6, 3], right.at[7, 3], at(dy=2))
    for a in range(3):
        got[5, a].wait_recv()
        got[7, a] = push(right.at[5, a], right.at[7, a], at(dx=3))
    z_second[0, 1].wait_recv()
    z_second[1, 1].wait_recv()
    sib.append(push(left.at[rb_2, 1], left.at[rb_2, 1], at(dc=1)))
    got[5, 3].wait_recv()
    prepare(5)
    mix(5)
    for a in range(4):
        got[3, a].wait_recv()
    prepare(3)
    mix(3)
    for copy in sib:
        copy.wait_recv()
    for slot in (0, 1, 2, 4, 5, 3):
        multiply(slot, 0)
        multiply(slot, 1)
    for a in range(3):
        got[6, a].wait_recv()
    prepare(6)
    mix(6)
    multiply(6, 0)
    multiply(6, 1)
    for a in range(4):
        got[7, a].wait_recv()
    prepare(7)
    mix(7)
    multiply(7, 1)
    sums = [
        push(part.at[2], part_in.at[0], dev_a),
        push(part.at[3], part_in.at[1], dev_b),
    ]
    multiply(7, 0)

    for g in range(2):
        sums[g].wait_recv()
        lanes = slice(g * 128, g * 128 + 128)
        for comp in range(2):
            for ip in range(4):
                cut = slice(ip * 128, ip * 128 + 128)
                even, odd = half_swap(
                    part[g, comp, 0:64, cut] + part_in[g, comp, 0:64, cut],
                    part[g, comp, 64:128, cut] + part_in[g, comp, 64:128, cut],
                    lower,
                )
                lo = slice(ip * 128, ip * 128 + 64)
                hi_rows = slice(ip * 128 + 64, ip * 128 + 128)
                if comp == 0:
                    out_i[lo, lanes] -= even
                    out_i[hi_rows, lanes] -= odd
                else:
                    out_r[lo, lanes] += even
                    out_r[hi_rows, lanes] += odd
    for copy in sent:
        copy.wait_send()


def on_device(g2_re, g2_im, g1_re, g1_im, hop_re, hop_im, coupling):
    vmem = pl.BlockSpec(memory_space=pltpu.VMEM)
    smem = pl.BlockSpec(memory_space=pltpu.SMEM)
    count = 72
    return pl.pallas_call(
        kernel,
        out_shape=(
            jax.ShapeDtypeStruct((512, 256), F32),
            jax.ShapeDtypeStruct((512, 256), F32),
            jax.ShapeDtypeStruct((64, 64), F32),
            jax.ShapeDtypeStruct((64, 64), F32),
        ),
        in_specs=[vmem] * 7 + [smem] * 2,
        out_specs=(vmem,) * 4,
        scratch_shapes=[
            pltpu.VMEM((8, 4, 2, 64, 512), F32),
            pltpu.VMEM((8, 2, 2, 256, 256), F32),
            pltpu.VMEM((2, 2, 128, 256), F32),
            pltpu.VMEM((8, 1024, 512), BF16),
            pltpu.VMEM((2, 256, 1024), BF16),
            pltpu.VMEM((4, 2, 128, 512), F32),
            pltpu.VMEM((2, 2, 128, 512), F32),
            pltpu.VMEM((4, 16, 128), F32),
            pltpu.VMEM((4, 16, 128), F32),
            pltpu.VMEM((2, 4, 16, 128), F32),
            pltpu.VMEM((2, 64, 512), F32),
            pltpu.VMEM((2, 256, 256), F32),
            pltpu.VMEM((64, 256), F32),
            pltpu.SemaphoreType.DMA((count,)),
            pltpu.SemaphoreType.DMA((count,)),
        ],
        compiler_params=pltpu.CompilerParams(
            collective_id=0, has_side_effects=True, vmem_limit_bytes=56 * 2**20
        ),
    )(g2_re, g2_im, g1_re, g1_im, hop_re, hop_im, coupling, hop_re, hop_im)


def solution(mesh):
    pairs = P("prow", ("pcol", "orb"))
    return jax.shard_map(
        on_device,
        mesh=mesh,
        in_specs=(pairs, pairs, pairs, pairs, P(), P(), P()),
        out_specs=(pairs, pairs, P(), P()),
        check_vma=False,
    )
```

```python
import functools

import jax
import jax.numpy as jnp
from jax import lax
from jax.experimental import pallas as pl
from jax.experimental.pallas import tpu as pltpu
from jax.sharding import PartitionSpec as P

HIGH = lax.Precision.HIGHEST
MESH = pl.DeviceIdType.MESH
F32 = jnp.float32
BF16 = jnp.bfloat16

ORB = 64
ROWS = 8
COLS = 4


def dot(a, b):
    return jnp.dot(a, b, precision=HIGH, preferred_element_type=F32)


def mxu(a, b):
    return jnp.dot(a, b, preferred_element_type=F32)


def iota(shape, dim):
    return lax.broadcasted_iota(jnp.int32, shape, dim)


def split(value):
    high = value.astype(BF16)
    return high, (value - high.astype(F32)).astype(BF16)


def half_swap(first, second, lower):
    return (
        jnp.where(lower, first, pltpu.roll(second, 64, 1)),
        jnp.where(lower, pltpu.roll(first, 64, 1), second),
    )


def kernel(
    g2r,
    g2i,
    g1r,
    g1i,
    hop_r,
    hop_i,
    coup,
    hop_r_s,
    hop_i_s,
    out_r,
    out_i,
    d1_r,
    d1_i,
    right,
    left,
    left_send,
    stack,
    lsplit,
    part,
    part_in,
    small_y,
    small_x,
    small_z,
    field_rows,
    kron,
    wide,
    send,
    recv,
):
    prow, pcol, orb = (lax.axis_index(n) for n in ("prow", "pcol", "orb"))
    z, c = prow // 2, prow % 2
    x = pcol % 4
    y = (pcol // 4) * 2 + orb
    rb = prow

    def at(dx=0, dy=0, dz=0, dc=0):
        xx, yy, zz, cc = (x + dx) % 4, (y + dy) % 4, (z + dz) % 4, (c + dc) % 2
        return (zz * 2 + cc, (yy // 2) * 4 + xx, yy % 2)

    def col_block(xx, yy):
        return (yy // 2) * 8 + xx * 2 + yy % 2

    cb = col_block(x, y)
    ya = y + 1 - 2 * orb
    yb = (y + 3 + 2 * orb) % 4
    dev_a = (prow, (ya // 2) * 4 + x, ya % 2)
    dev_b = (prow, (yb // 2) * 4 + x, yb % 2)

    partners = [
        at(dc=1),
        at(dx=1),
        at(dx=3),
        at(dx=2),
        at(dy=1),
        at(dy=3),
        at(dy=2),
        at(dz=1),
        at(dz=3),
        at(dz=2),
    ]
    barrier = pltpu.get_barrier_semaphore()
    for device in partners:
        pl.semaphore_signal(barrier, inc=1, device_id=device, device_id_type=MESH)

    sent = []

    def push(src, dst, device):
        n = len(sent)
        copy = pltpu.make_async_remote_copy(
            src_ref=src,
            dst_ref=dst,
            send_sem=send.at[n],
            recv_sem=recv.at[n],
            device_id=device,
            device_id_type=MESH,
        )
        copy.start()
        sent.append(copy)
        return copy

    lower = iota((64, 128), 1) < 64
    for ch in range(2):
        for comp, g in ((0, g2r), (1, g2i)):
            for kt in range(2):
                lanes = slice(kt * 128, kt * 128 + 128)
                for ip in range(2):
                    top = ch * 256 + ip * 128
                    even, odd = half_swap(
                        g[top : top + 64, lanes], g[top + 64 : top + 128, lanes], lower
                    )
                    to = slice(ip * 128, ip * 128 + 128)
                    right[0, ch, 4 * kt + comp, :, to] = even
                    right[0, ch, 4 * kt + 2 + comp, :, to] = odd
    for comp in range(2):
        for k in range(4):
            left[rb, 0, comp, k * 64 : k * 64 + 64, :] = right[0, orb, 2 * k + comp]
            left_send[k // 2, comp, (k % 2) * 64 : (k % 2) * 64 + 64, :] = right[
                0, 1 - orb, 2 * k + comp
            ]

    pl.semaphore_wait(barrier, len(partners))

    got = {}

    def go(to, start, ch, first, last, device):
        cut = pl.ds(first, last - first)
        got[to, ch, first] = push(right.at[start, ch, cut], right.at[to, ch, cut], device)

    def arrived(slot, ch, *firsts):
        for first in firsts:
            got[slot, ch, first].wait_recv()

    def own_y(ch, first, last):
        go(1, 0, ch, first, last, at(dy=2))

    def own_x(ch, first, last):
        go(6, 0, ch, first, last, at(dx=1))
        go(2, 0, ch, first, last, at(dx=3))

    own_y(0, 0, 3)
    own_x(0, 6, 8)
    own_x(0, 0, 6)
    pre = [
        push(left_send.at[0], left.at[rb, 1, :, 0:128, :], dev_a),
        push(left_send.at[1], left.at[rb, 1, :, 128:256, :], dev_b),
    ]
    z_first = {}
    for d, name in ((1, "m"), (3, "p")):
        z_first[name, 0] = push(left.at[rb, 0], left.at[rb, 0], at(dz=d))
    own_y(0, 3, 6)
    own_y(0, 6, 8)
    own_x(1, 6, 8)
    sib = {(0, 0): push(left.at[rb, 0], left.at[rb, 0], at(dc=1))}

    same = iota((64, 256), 0) == iota((64, 256), 1) % 64
    repeat = same.astype(F32)
    wide[...] = dot(coup[...], repeat)
    diag_r = jnp.concatenate(
        [jnp.sum(jnp.where(same, g2r[i * 64 : i * 64 + 64, :], 0.0), 0, keepdims=True) for i in range(ROWS)], 0
    )
    diag_i = jnp.concatenate(
        [jnp.sum(jnp.where(same, g2i[i * 64 : i * 64 + 64, :], 0.0), 0, keepdims=True) for i in range(ROWS)], 0
    )
    weight = wide[pl.ds(pl.multiple_of(rb * ROWS, ROWS), ROWS), :]
    place = iota((256, 128), 1) - COLS * cb
    group = iota((256, 128), 0) // 64
    to_re = (place == group).astype(F32)
    to_im = (place == group + 64).astype(F32)
    small_y[0, 8:16, :] = dot(weight * diag_i, to_re) - dot(weight * diag_r, to_im)
    spot = iota((8, 128), 1) - COLS * cb
    eye8 = iota((8, 8), 0) == iota((8, 8), 1)
    tile = jnp.zeros((8, 128), F32)
    for q in range(COLS):
        for lane, g1 in ((q, g1r), (q + 64, g1i)):
            column = jnp.sum(jnp.where(eye8, g1[q : q + 1, :], 0.0), 1, keepdims=True)
            tile = tile + jnp.where(spot == lane, column, 0.0)
    small_y[0, 0:8, :] = tile

    tiny_y = [
        push(small_y.at[0], small_y.at[n], at(dy=d)) for n, d in ((1, 1), (2, 3), (3, 2))
    ]

    eye = (iota((64, 64), 0) == iota((64, 64), 1)).astype(F32)
    hr, hi = hop_r[...], hop_i[...]
    off_r = 0.5 * (hr + hr.T) * (1.0 - eye)
    off_i = 0.5 * (hi - hi.T)
    choose = (iota((64, 512), 0) == rb * ROWS + iota((64, 512), 1) // 64).astype(F32)
    field_rows[0] = dot(off_r, choose)
    field_rows[1] = -dot(off_i, choose)
    block_diag = iota((256, 256), 0) // 64 == iota((256, 256), 1) // 64
    tall = (iota((256, 64), 0) % 64 == iota((256, 64), 1)).astype(F32)
    kron[0] = jnp.where(block_diag, dot(tall, dot(off_r, repeat)), 0.0)
    kron[1] = jnp.where(block_diag, dot(tall, dot(off_i, repeat)), 0.0)
    coup_t = coup[...].T

    def where_is(slot):
        return (x + slot // 2) % 4, (y + 2 * (slot % 2)) % 4

    for ch in range(2):
        for g in range(4):
            part[ch, g] = jnp.zeros((2, 128, 256), F32)

    def prepare(slot, ch):
        base = col_block(*where_is(slot)) * COLS
        match = iota((64, 256), 0) == iota((64, 256), 1) % 64
        for a in range(4):
            v = jnp.sum(
                jnp.where(iota((64, 64), 1) == base + a, coup_t, 0.0), 1, keepdims=True
            )
            for comp in range(2):
                value = v * right[slot, ch, 2 * a + comp] + jnp.where(
                    match,
                    field_rows[comp, pl.ds(base + a, 1), ch * 256 : ch * 256 + 256],
                    0.0,
                )
                for n, term in enumerate(split(value)):
                    row = n * 768 + (1 - comp) * 256 + a * 64
                    stack[slot, ch, row : row + 64, :] = term
                    if comp == 1:
                        stack[slot, ch, row + 512 : row + 576, :] = -term

    def mix(slot, ch):
        base = col_block(*where_is(slot)) * COLS
        starts = (cb * COLS, col_block(x, ya) * COLS, col_block(x, yb) * COLS)
        for kk in range(8):
            k = starts[0] + kk if kk < 4 else starts[1 if kk < 6 else 2] + kk - 4
            scale = []
            for a in range(4):
                sr = 0.5 * (hop_r_s[base + a, k] + hop_r_s[k, base + a])
                si = 0.5 * (hop_i_s[base + a, k] - hop_i_s[k, base + a])
                sr = jnp.where(k == base + a, 0.0, sr)
                scale.append((jnp.full((8, 256), sr, F32), jnp.full((8, 256), si, F32)))
            for strip in range(8):
                to = slice((kk % 2) * 64 + strip * 8, (kk % 2) * 64 + strip * 8 + 8)
                rows = slice(strip * 8, strip * 8 + 8)
                acc_r = part[ch, kk // 2, 0, to, :]
                acc_i = part[ch, kk // 2, 1, to, :]
                for a in range(4):
                    sr, si = scale[a]
                    tr = right[slot, ch, 2 * a, rows, :]
                    ti = right[slot, ch, 2 * a + 1, rows, :]
                    acc_r += si * ti - sr * tr
                    acc_i -= sr * ti + si * tr
                part[ch, kk // 2, 0, to, :] = acc_r
                part[ch, kk // 2, 1, to, :] = acc_i

    def enter(ch, first, count=1, stride=1):
        @pl.loop(0, count)
        def _(n):
            prepare(first + n * stride, ch)
            mix(first + n * stride, ch)

    def split_left(which, p):
        @pl.loop(0, 4)
        def _(step):
            rows = pl.ds(pl.multiple_of(step * 64, 64), 64)
            to = pl.ds(pl.multiple_of(p * 256 + step * 64, 64), 64)
            for comp in range(2):
                for n, term in enumerate(split(left[which, p, comp, rows, :])):
                    lane = n * 512 + comp * 256
                    lsplit[which, to, lane : lane + 256] = term

    def multiply(slot, ch, halves=(0, 1)):
        xx, yy = where_is(slot)
        which = (yy // 2) * 4 + xx
        rows = slice(halves[0] * 256, halves[-1] * 256 + 256)

        @pl.loop(0, 2)
        def _(comp):
            start = (1 - comp) * 256
            high = stack[slot, ch, pl.ds(pl.multiple_of(start, 256), 512), :]
            low = stack[slot, ch, pl.ds(pl.multiple_of(start + 768, 256), 512), :]
            value = (
                mxu(lsplit[which, rows, 0:512], high)
                + mxu(lsplit[which, rows, 0:512], low)
                + mxu(lsplit[which, rows, 512:1024], high)
            )
            for n in range(2 * len(halves)):
                part[ch, 2 * halves[0] + n, comp] += value[n * 128 : n * 128 + 128]

    def slot_of(zz, cc):
        return ((2 * (zz % 2) + cc - x + 4) % 4) * 2 + (zz // 2 + y // 2) % 2

    def along_x(ch, first):
        arrived(1, ch, first)
        go(7, 1, ch, first, first + 3, at(dx=1))
        go(3, 1, ch, first, first + 3, at(dx=3))

    def relay_few(ch):
        arrived(6, ch, 6)
        arrived(2, ch, 6)
        go(4, 6, ch, 6, 7, at(dx=1))
        go(4, 2, ch, 7, 8, at(dx=3))
        go(7, 6, ch, 6, 8, at(dy=2))
        go(3, 2, ch, 6, 8, at(dy=2))

    def relay(ch):
        arrived(6, ch, 0)
        go(4, 6, ch, 0, 6, at(dx=1))
        arrived(2, ch, 0)

    def relay_far(ch):
        arrived(4, ch, 6, 7)
        go(5, 4, ch, 6, 8, at(dy=2))

    def relay_last(ch, first):
        arrived(3, ch, first)
        go(5, 3, ch, first, first + 3, at(dx=3))

    rb_m = ((z + 3) % 4) * 2 + c
    rb_p = ((z + 1) % 4) * 2 + c
    rb_2 = ((z + 2) % 4) * 2 + c
    z_second = {}

    def pass_on(p):
        z_first["m", p].wait_recv()
        z_second[0, p] = push(left.at[rb_m, p, 0], left.at[rb_m, p, 0], at(dz=1))
        sib[3, p] = push(left.at[rb_m, p], left.at[rb_m, p], at(dc=1))
        z_first["p", p].wait_recv()
        z_second[1, p] = push(left.at[rb_p, p, 1], left.at[rb_p, p, 1], at(dz=3))
        sib[1, p] = push(left.at[rb_p, p], left.at[rb_p, p], at(dc=1))

    def pass_far(p):
        z_second[0, p].wait_recv()
        z_second[1, p].wait_recv()
        sib[2, p] = push(left.at[rb_2, p], left.at[rb_2, p], at(dc=1))
        split_left(rb_2, p)

    def from_sibling(dz):
        for p in range(2):
            sib[dz, p].wait_recv()
            split_left(((z + dz) % 4) * 2 + 1 - c, p)

    def by_left(dz):
        @pl.loop(0, 2)
        def _(cc):
            multiply(slot_of((z + dz) % 4, cc), 0)

    def times(first, count, stride, halves=(0, 1)):
        @pl.loop(0, count)
        def _(n):
            multiply(first + n * stride, 1, halves)

    sums = {}

    def send_sums(ch):
        sums[ch, 0] = push(part.at[ch, 2], part_in.at[ch, 0], dev_a)
        sums[ch, 1] = push(part.at[ch, 3], part_in.at[ch, 1], dev_b)

    along_x(0, 0)
    enter(0, 0)
    for copy in pre:
        copy.wait_recv()
    for d, name in ((1, "m"), (3, "p")):
        z_first[name, 1] = push(left.at[rb, 1], left.at[rb, 1], at(dz=d))
    sib[0, 1] = push(left.at[rb, 1], left.at[rb, 1], at(dc=1))
    relay_few(0)
    relay(0)
    along_x(0, 3)
    pass_on(0)
    own_y(1, 0, 3)
    own_y(1, 3, 6)
    own_y(1, 6, 8)
    for copy in tiny_y:
        copy.wait_recv()
    small_x[0] = small_y[0] + small_y[1] + small_y[2] + small_y[3]
    tiny_x = [
        push(small_x.at[0], small_x.at[n], at(dx=d)) for n, d in ((1, 1), (2, 3), (3, 2))
    ]
    split_left(rb, 0)
    split_left(rb, 1)
    split_left(rb_m, 0)
    split_left(rb_p, 0)
    arrived(1, 0, 6)
    enter(0, 1)
    relay_last(0, 0)
    enter(0, 2, 2, 4)
    relay_last(0, 3)
    own_x(1, 0, 6)
    relay_far(0)
    pass_on(1)
    for copy in tiny_x:
        copy.wait_recv()
    small_z[c, z] = small_x[0] + small_x[1] + small_x[2] + small_x[3]
    tiny_z = [
        push(small_z.at[c, z], small_z.at[c, z], at(dz=d)) for d in (1, 3, 2)
    ]
    along_x(1, 0)
    along_x(1, 3)
    split_left(rb_m, 1)
    split_left(rb_p, 1)
    arrived(3, 0, 6)
    arrived(7, 0, 0, 3, 6)
    enter(0, 3, 2, 4)
    from_sibling(0)
    enter(1, 0)
    arrived(1, 1, 6)
    enter(1, 1)
    pass_far(0)
    from_sibling(3)
    from_sibling(1)
    arrived(4, 0, 0)
    arrived(5, 0, 0, 3, 6)
    enter(0, 4, 2)
    by_left(0)
    by_left(3)
    by_left(1)
    for copy in tiny_z:
        copy.wait_recv()
    tiny_c = push(small_z.at[c], small_z.at[c], at(dc=1))
    pass_far(1)
    from_sibling(2)
    by_left(2)
    send_sums(0)
    relay_few(1)
    relay(1)
    enter(1, 2, 2, 4)
    times(0, 2, 1)
    relay_last(1, 0)
    times(2, 2, 4)
    relay_last(1, 3)
    relay_far(1)
    arrived(3, 1, 6)
    arrived(7, 1, 0, 3, 6)
    enter(1, 3, 2, 4)
    times(3, 2, 4)
    arrived(4, 1, 0)
    arrived(5, 1, 0, 3, 6)
    enter(1, 4, 2)
    times(4, 2, 1, (1,))
    send_sums(1)
    times(4, 2, 1, (0,))
    tiny_c.wait_recv()

    for half in range(2):
        rows = slice(half * 256, half * 256 + 256)
        gr, gi = g2r[rows, :], g2i[rows, :]
        kr, ki = kron[0], kron[1]
        out_r[rows, :] = dot(kr, gi) + dot(ki, gr) - dot(gr, ki) - dot(gi, kr)
        out_i[rows, :] = dot(ki, gi) - dot(kr, gr) + dot(gr, kr) - dot(gi, ki)

    rows_z = [(r // 2, r % 2) for r in range(8)]
    one = jnp.concatenate([small_z[cc, zz, 0:8, :] for zz, cc in rows_z], 0)
    coll = jnp.concatenate([small_z[cc, zz, 8:16, :] for zz, cc in rows_z], 0)
    gr, gi = one[:, 0:64], one[:, 64:128]
    cr, ci = coll[:, 0:64], coll[:, 64:128]
    density = jnp.sum(gr * eye, 0, keepdims=True)
    hartree_col = jnp.sum(coup[...] * density, 1, keepdims=True)
    diag_col = hartree_col + jnp.sum(hr * eye, 1, keepdims=True)
    diag_row = jnp.sum(diag_col * eye, 0, keepdims=True)
    fr = off_r + diag_col * eye
    fi = off_i
    comm_r = dot(fr, gr) - dot(fi, gi) - dot(gr, fr) + dot(gi, fi)
    comm_i = dot(fr, gi) + dot(fi, gr) - dot(gr, fi) - dot(gi, fr)
    d1_r[...] = comm_i + cr + cr.T
    d1_i[...] = ci - ci.T - comm_r

    from_cols = jnp.zeros((1, 256), F32)
    lane_group = iota((1, 256), 1) // 64
    row64 = iota((64, 64), 0)
    table = coup[...] + diag_col + diag_row
    table_wide = dot(table, repeat)
    row_wide = iota((64, 256), 0)
    for k in range(COLS):
        picked = jnp.sum(
            jnp.where(row_wide == cb * COLS + k, table_wide, 0.0), 0, keepdims=True
        )
        from_cols = jnp.where(lane_group == k, picked, from_cols)
    table_t = coup_t + diag_col + diag_row
    for i in range(ROWS):
        from_rows = jnp.sum(
            jnp.where(iota((64, 64), 1) == rb * ROWS + i, table_t, 0.0), 1, keepdims=True
        )
        rows = slice(i * 64, i * 64 + 64)
        factor = from_rows - from_cols
        out_r[rows, :] += factor * g2i[rows, :]
        out_i[rows, :] -= factor * g2r[rows, :]

    for ch in range(2):
        for g in range(2):
            sums[ch, g].wait_recv()
            lanes = slice(g * 128, g * 128 + 128)
            for comp in range(2):
                for ip in range(2):
                    cut = slice(ip * 128, ip * 128 + 128)
                    even, odd = half_swap(
                        part[ch, g, comp, 0:64, cut] + part_in[ch, g, comp, 0:64, cut],
                        part[ch, g, comp, 64:128, cut] + part_in[ch, g, comp, 64:128, cut],
                        lower,
                    )
                    top = ch * 256 + ip * 128
                    for first, value in ((top, even), (top + 64, odd)):
                        if comp == 0:
                            out_i[first : first + 64, lanes] -= value
                        else:
                            out_r[first : first + 64, lanes] += value
    for copy in sent:
        copy.wait_send()


def on_device(g2_re, g2_im, g1_re, g1_im, hop_re, hop_im, coupling):
    vmem = pl.BlockSpec(memory_space=pltpu.VMEM)
    smem = pl.BlockSpec(memory_space=pltpu.SMEM)
    count = 72
    return pl.pallas_call(
        kernel,
        out_shape=(
            jax.ShapeDtypeStruct((512, 256), F32),
            jax.ShapeDtypeStruct((512, 256), F32),
            jax.ShapeDtypeStruct((64, 64), F32),
            jax.ShapeDtypeStruct((64, 64), F32),
        ),
        in_specs=[vmem] * 7 + [smem] * 2,
        out_specs=(vmem,) * 4,
        scratch_shapes=[
            pltpu.VMEM((8, 2, 8, 64, 256), F32),
            pltpu.VMEM((8, 2, 2, 256, 256), F32),
            pltpu.VMEM((2, 2, 128, 256), F32),
            pltpu.VMEM((8, 2, 1536, 256), BF16),
            pltpu.VMEM((8, 512, 1024), BF16),
            pltpu.VMEM((2, 4, 2, 128, 256), F32),
            pltpu.VMEM((2, 2, 2, 128, 256), F32),
            pltpu.VMEM((4, 16, 128), F32),
            pltpu.VMEM((4, 16, 128), F32),
            pltpu.VMEM((2, 4, 16, 128), F32),
            pltpu.VMEM((2, 64, 512), F32),
            pltpu.VMEM((2, 256, 256), F32),
            pltpu.VMEM((64, 256), F32),
            pltpu.SemaphoreType.DMA((count,)),
            pltpu.SemaphoreType.DMA((count,)),
        ],
        compiler_params=pltpu.CompilerParams(
            collective_id=0, has_side_effects=True, vmem_limit_bytes=56 * 2**20
        ),
    )(g2_re, g2_im, g1_re.T, g1_im.T, hop_re, hop_im, coupling, hop_re, hop_im)


def solution(mesh):
    pairs = P("prow", ("pcol", "orb"))
    return jax.shard_map(
        on_device,
        mesh=mesh,
        in_specs=(pairs, pairs, pairs, pairs, P(), P(), P()),
        out_specs=(pairs, pairs, P(), P()),
        check_vma=False,
    )
```

```python
import functools

import jax
import jax.numpy as jnp
from jax import lax
from jax.experimental import pallas as pl
from jax.experimental.pallas import tpu as pltpu
from jax.sharding import PartitionSpec as P

HIGH = lax.Precision.HIGHEST
MESH = pl.DeviceIdType.MESH
F32 = jnp.float32
BF16 = jnp.bfloat16

ORB = 64
ROWS = 8
COLS = 4


def dot(a, b):
    return jnp.dot(a, b, precision=HIGH, preferred_element_type=F32)


def mxu(a, b):
    return jnp.dot(a, b, preferred_element_type=F32)


def iota(shape, dim):
    return lax.broadcasted_iota(jnp.int32, shape, dim)


def split(value):
    high = value.astype(BF16)
    return high, (value - high.astype(F32)).astype(BF16)


def half_swap(first, second, lower):
    return (
        jnp.where(lower, first, pltpu.roll(second, 64, 1)),
        jnp.where(lower, pltpu.roll(first, 64, 1), second),
    )


def kernel(
    g2r,
    g2i,
    g1r,
    g1i,
    hop_r,
    hop_i,
    coup,
    hop_r_s,
    hop_i_s,
    out_r,
    out_i,
    d1_r,
    d1_i,
    right,
    left,
    left_send,
    stack,
    lsplit,
    part,
    part_in,
    small_y,
    small_x,
    small_z,
    field_rows,
    kron,
    wide,
    send,
    recv,
):
    prow, pcol, orb = (lax.axis_index(n) for n in ("prow", "pcol", "orb"))
    z, c = prow // 2, prow % 2
    x = pcol % 4
    y = (pcol // 4) * 2 + orb
    rb = prow

    def at(dx=0, dy=0, dz=0, dc=0):
        xx, yy, zz, cc = (x + dx) % 4, (y + dy) % 4, (z + dz) % 4, (c + dc) % 2
        return (zz * 2 + cc, (yy // 2) * 4 + xx, yy % 2)

    def col_block(xx, yy):
        return (yy // 2) * 8 + xx * 2 + yy % 2

    cb = col_block(x, y)
    ya = y + 1 - 2 * orb
    yb = (y + 3 + 2 * orb) % 4
    dev_a = (prow, (ya // 2) * 4 + x, ya % 2)
    dev_b = (prow, (yb // 2) * 4 + x, yb % 2)

    partners = [
        at(dc=1),
        at(dx=1),
        at(dx=3),
        at(dx=2),
        at(dy=1),
        at(dy=3),
        at(dy=2),
        at(dz=1),
        at(dz=3),
        at(dz=2),
    ]
    barrier = pltpu.get_barrier_semaphore()
    for device in partners:
        pl.semaphore_signal(barrier, inc=1, device_id=device, device_id_type=MESH)

    sent = []

    def push(src, dst, device):
        n = len(sent)
        copy = pltpu.make_async_remote_copy(
            src_ref=src,
            dst_ref=dst,
            send_sem=send.at[n],
            recv_sem=recv.at[n],
            device_id=device,
            device_id_type=MESH,
        )
        copy.start()
        sent.append(copy)
        return copy

    lower = iota((64, 128), 1) < 64
    for ch in range(2):
        for comp, g in ((0, g2r), (1, g2i)):
            for kt in range(2):
                lanes = slice(kt * 128, kt * 128 + 128)
                for ip in range(2):
                    top = ch * 256 + ip * 128
                    even, odd = half_swap(
                        g[top : top + 64, lanes], g[top + 64 : top + 128, lanes], lower
                    )
                    to = slice(ip * 128, ip * 128 + 128)
                    right[0, ch, 4 * kt + comp, :, to] = even
                    right[0, ch, 4 * kt + 2 + comp, :, to] = odd
    for comp in range(2):
        for k in range(4):
            left[rb, 0, comp, k * 64 : k * 64 + 64, :] = right[0, orb, 2 * k + comp]
            left_send[k // 2, comp, (k % 2) * 64 : (k % 2) * 64 + 64, :] = right[
                0, 1 - orb, 2 * k + comp
            ]

    pl.semaphore_wait(barrier, len(partners))

    got = {}

    def go(to, start, ch, first, last, device):
        cut = pl.ds(first, last - first)
        got[to, ch, first] = push(right.at[start, ch, cut], right.at[to, ch, cut], device)

    def arrived(slot, ch, *firsts):
        for first in firsts:
            got[slot, ch, first].wait_recv()

    def own_y(ch, first, last):
        go(1, 0, ch, first, last, at(dy=2))

    def own_x(ch, first, last):
        go(6, 0, ch, first, last, at(dx=1))
        go(2, 0, ch, first, last, at(dx=3))

    own_y(0, 0, 4)
    own_x(0, 6, 8)
    own_x(0, 0, 6)
    pre = [
        push(left_send.at[0], left.at[rb, 1, :, 0:128, :], dev_a),
        push(left_send.at[1], left.at[rb, 1, :, 128:256, :], dev_b),
    ]
    z_first = {}
    for d, name in ((1, "m"), (3, "p")):
        z_first[name, 0] = push(left.at[rb, 0], left.at[rb, 0], at(dz=d))
    own_y(0, 4, 6)
    own_y(0, 6, 8)
    own_x(1, 6, 8)
    sib = {(0, 0): push(left.at[rb, 0], left.at[rb, 0], at(dc=1))}

    same = iota((64, 256), 0) == iota((64, 256), 1) % 64
    repeat = same.astype(F32)
    wide[...] = dot(coup[...], repeat)
    diag_r = jnp.concatenate(
        [jnp.sum(jnp.where(same, g2r[i * 64 : i * 64 + 64, :], 0.0), 0, keepdims=True) for i in range(ROWS)], 0
    )
    diag_i = jnp.concatenate(
        [jnp.sum(jnp.where(same, g2i[i * 64 : i * 64 + 64, :], 0.0), 0, keepdims=True) for i in range(ROWS)], 0
    )
    weight = wide[pl.ds(pl.multiple_of(rb * ROWS, ROWS), ROWS), :]
    place = iota((256, 128), 1) - COLS * cb
    group = iota((256, 128), 0) // 64
    to_re = (place == group).astype(F32)
    to_im = (place == group + 64).astype(F32)
    small_y[0, 8:16, :] = dot(weight * diag_i, to_re) - dot(weight * diag_r, to_im)
    spot = iota((8, 128), 1) - COLS * cb
    eye8 = iota((8, 8), 0) == iota((8, 8), 1)
    tile = jnp.zeros((8, 128), F32)
    for q in range(COLS):
        for lane, g1 in ((q, g1r), (q + 64, g1i)):
            column = jnp.sum(jnp.where(eye8, g1[q : q + 1, :], 0.0), 1, keepdims=True)
            tile = tile + jnp.where(spot == lane, column, 0.0)
    small_y[0, 0:8, :] = tile

    tiny_y = [
        push(small_y.at[0], small_y.at[n], at(dy=d)) for n, d in ((1, 1), (2, 3), (3, 2))
    ]

    eye = (iota((64, 64), 0) == iota((64, 64), 1)).astype(F32)
    hr, hi = hop_r[...], hop_i[...]
    off_r = 0.5 * (hr + hr.T) * (1.0 - eye)
    off_i = 0.5 * (hi - hi.T)
    choose = (iota((64, 512), 0) == rb * ROWS + iota((64, 512), 1) // 64).astype(F32)
    field_rows[0] = dot(off_r, choose)
    field_rows[1] = -dot(off_i, choose)
    block_diag = iota((256, 256), 0) // 64 == iota((256, 256), 1) // 64
    tall = (iota((256, 64), 0) % 64 == iota((256, 64), 1)).astype(F32)
    kron[0] = jnp.where(block_diag, dot(tall, dot(off_r, repeat)), 0.0)
    kron[1] = jnp.where(block_diag, dot(tall, dot(off_i, repeat)), 0.0)
    coup_t = coup[...].T

    def where_is(slot):
        return (x + slot // 2) % 4, (y + 2 * (slot % 2)) % 4

    for ch in range(2):
        for g in range(4):
            part[ch, g] = jnp.zeros((2, 128, 256), F32)

    def prepare(slot, ch, parts):
        base = col_block(*where_is(slot)) * COLS
        match = iota((64, 256), 0) == iota((64, 256), 1) % 64
        for a in parts:
            v = jnp.sum(
                jnp.where(iota((64, 64), 1) == base + a, coup_t, 0.0), 1, keepdims=True
            )
            for comp in range(2):
                value = v * right[slot, ch, 2 * a + comp] + jnp.where(
                    match,
                    field_rows[comp, pl.ds(base + a, 1), ch * 256 : ch * 256 + 256],
                    0.0,
                )
                for n, term in enumerate(split(value)):
                    row = n * 768 + (1 - comp) * 256 + a * 64
                    stack[slot, ch, row : row + 64, :] = term
                    if comp == 1:
                        stack[slot, ch, row + 512 : row + 576, :] = -term

    def mix(slot, ch, parts):
        base = col_block(*where_is(slot)) * COLS
        starts = (cb * COLS, col_block(x, ya) * COLS, col_block(x, yb) * COLS)
        for kk in range(8):
            k = starts[0] + kk if kk < 4 else starts[1 if kk < 6 else 2] + kk - 4
            scale = {}
            for a in parts:
                sr = 0.5 * (hop_r_s[base + a, k] + hop_r_s[k, base + a])
                si = 0.5 * (hop_i_s[base + a, k] - hop_i_s[k, base + a])
                sr = jnp.where(k == base + a, 0.0, sr)
                scale[a] = jnp.full((8, 256), sr, F32), jnp.full((8, 256), si, F32)
            for strip in range(8):
                to = slice((kk % 2) * 64 + strip * 8, (kk % 2) * 64 + strip * 8 + 8)
                rows = slice(strip * 8, strip * 8 + 8)
                acc_r = part[ch, kk // 2, 0, to, :]
                acc_i = part[ch, kk // 2, 1, to, :]
                for a in parts:
                    sr, si = scale[a]
                    tr = right[slot, ch, 2 * a, rows, :]
                    ti = right[slot, ch, 2 * a + 1, rows, :]
                    acc_r += si * ti - sr * tr
                    acc_i -= sr * ti + si * tr
                part[ch, kk // 2, 0, to, :] = acc_r
                part[ch, kk // 2, 1, to, :] = acc_i

    def enter(ch, first, count=1, stride=1, parts=(0, 1, 2, 3)):
        @pl.loop(0, count)
        def _(n):
            prepare(first + n * stride, ch, parts)
            mix(first + n * stride, ch, parts)

    def split_left(which, p):
        @pl.loop(0, 4)
        def _(step):
            rows = pl.ds(pl.multiple_of(step * 64, 64), 64)
            to = pl.ds(pl.multiple_of(p * 256 + step * 64, 64), 64)
            for comp in range(2):
                for n, term in enumerate(split(left[which, p, comp, rows, :])):
                    lane = n * 512 + comp * 256
                    lsplit[which, to, lane : lane + 256] = term

    def multiply(slot, ch, halves=(0, 1)):
        xx, yy = where_is(slot)
        which = (yy // 2) * 4 + xx
        rows = slice(halves[0] * 256, halves[-1] * 256 + 256)

        @pl.loop(0, 2)
        def _(comp):
            start = (1 - comp) * 256
            high = stack[slot, ch, pl.ds(pl.multiple_of(start, 256), 512), :]
            low = stack[slot, ch, pl.ds(pl.multiple_of(start + 768, 256), 512), :]
            value = (
                mxu(lsplit[which, rows, 0:512], high)
                + mxu(lsplit[which, rows, 0:512], low)
                + mxu(lsplit[which, rows, 512:1024], high)
            )
            for n in range(2 * len(halves)):
                part[ch, 2 * halves[0] + n, comp] += value[n * 128 : n * 128 + 128]

    def slot_of(zz, cc):
        return ((2 * (zz % 2) + cc - x + 4) % 4) * 2 + (zz // 2 + y // 2) % 2

    def along_x(ch, first):
        arrived(1, ch, first)
        go(7, 1, ch, first, 4 + first // 2, at(dx=1))
        go(3, 1, ch, first, 4 + first // 2, at(dx=3))

    def relay_few_x(ch):
        arrived(6, ch, 6)
        arrived(2, ch, 6)
        go(4, 6, ch, 6, 7, at(dx=1))
        go(4, 2, ch, 7, 8, at(dx=3))

    def relay_few_y(ch):
        go(7, 6, ch, 6, 8, at(dy=2))
        go(3, 2, ch, 6, 8, at(dy=2))

    def relay(ch):
        arrived(6, ch, 0)
        go(4, 6, ch, 0, 4, at(dx=1))
        go(4, 6, ch, 4, 6, at(dx=1))
        arrived(2, ch, 0)

    def relay_far(ch):
        arrived(4, ch, 6, 7)
        go(5, 4, ch, 6, 8, at(dy=2))

    def relay_last(ch, first):
        arrived(3, ch, first)
        go(5, 3, ch, first, 4 + first // 2, at(dx=3))

    rb_m = ((z + 3) % 4) * 2 + c
    rb_p = ((z + 1) % 4) * 2 + c
    rb_2 = ((z + 2) % 4) * 2 + c
    z_second = {}

    def pass_on(p):
        z_first["m", p].wait_recv()
        z_second[0, p] = push(left.at[rb_m, p, 0], left.at[rb_m, p, 0], at(dz=1))
        sib[3, p] = push(left.at[rb_m, p], left.at[rb_m, p], at(dc=1))
        z_first["p", p].wait_recv()
        z_second[1, p] = push(left.at[rb_p, p, 1], left.at[rb_p, p, 1], at(dz=3))
        sib[1, p] = push(left.at[rb_p, p], left.at[rb_p, p], at(dc=1))

    def pass_far(p):
        z_second[0, p].wait_recv()
        z_second[1, p].wait_recv()
        sib[2, p] = push(left.at[rb_2, p], left.at[rb_2, p], at(dc=1))
        split_left(rb_2, p)

    def from_sibling(dz):
        for p in range(2):
            sib[dz, p].wait_recv()
            split_left(((z + dz) % 4) * 2 + 1 - c, p)

    def by_left(first, count, far):
        @pl.loop(0, count)
        def _(n):
            slot = slot_of((z + 3 + (first + n) // 2) % 4, n % 2)

            @pl.when((slot // 2 == 2) == far)
            def _():
                multiply(slot, 0)

    def times(first, count, stride, halves=(0, 1)):
        @pl.loop(0, count)
        def _(n):
            multiply(first + n * stride, 1, halves)

    sums = {}

    def send_sums(ch):
        sums[ch, 0] = push(part.at[ch, 2], part_in.at[ch, 0], dev_a)
        sums[ch, 1] = push(part.at[ch, 3], part_in.at[ch, 1], dev_b)

    relay_few_x(0)
    relay_few_y(0)
    enter(0, 0)
    along_x(0, 0)
    enter(1, 0)
    split_left(rb, 0)

    for half in range(2):
        rows = slice(half * 256, half * 256 + 256)
        gr, gi = g2r[rows, :], g2i[rows, :]
        kr, ki = kron[0], kron[1]
        out_r[rows, :] = dot(kr, gi) + dot(ki, gr) - dot(gr, ki) - dot(gi, kr)
        out_i[rows, :] = dot(ki, gi) - dot(kr, gr) + dot(gr, kr) - dot(gi, ki)

    for copy in pre:
        copy.wait_recv()
    for d, name in ((1, "m"), (3, "p")):
        z_first[name, 1] = push(left.at[rb, 1], left.at[rb, 1], at(dz=d))
    sib[0, 1] = push(left.at[rb, 1], left.at[rb, 1], at(dc=1))
    pass_on(0)
    split_left(rb, 1)
    along_x(0, 4)
    relay(0)
    relay_far(0)
    own_y(1, 0, 4)
    own_y(1, 4, 6)
    relay_few_x(1)
    relay_few_y(1)
    own_y(1, 6, 8)
    split_left(rb_m, 0)
    split_left(rb_p, 0)
    arrived(1, 0, 6)
    enter(0, 1)
    enter(0, 2, 2, 4)
    relay_last(0, 0)
    for copy in tiny_y:
        copy.wait_recv()
    small_x[0] = small_y[0] + small_y[1] + small_y[2] + small_y[3]
    tiny_x = [
        push(small_x.at[0], small_x.at[n], at(dx=d)) for n, d in ((1, 1), (2, 3), (3, 2))
    ]
    relay_last(0, 4)
    own_x(1, 0, 6)
    arrived(3, 0, 6)
    arrived(7, 0, 0, 4, 6)
    enter(0, 3, 2, 4)
    pass_on(1)
    from_sibling(0)
    split_left(rb_m, 1)
    split_left(rb_p, 1)
    from_sibling(3)
    from_sibling(1)
    by_left(0, 6, False)
    along_x(1, 0)
    along_x(1, 4)
    relay_far(1)
    arrived(4, 0, 0, 4)
    arrived(5, 0, 0, 4, 6)
    enter(0, 4, 2)
    by_left(0, 6, True)
    for copy in tiny_x:
        copy.wait_recv()
    small_z[c, z] = small_x[0] + small_x[1] + small_x[2] + small_x[3]
    tiny_z = [
        push(small_z.at[c, z], small_z.at[c, z], at(dz=d)) for d in (1, 3, 2)
    ]
    pass_far(0)
    pass_far(1)
    from_sibling(2)
    by_left(6, 2, False)
    by_left(6, 2, True)
    send_sums(0)
    relay(1)
    arrived(1, 1, 6)
    enter(1, 1)
    enter(1, 2, 2, 4)
    times(0, 2, 1)
    relay_last(1, 0)
    times(2, 2, 4)
    relay_last(1, 4)
    for copy in tiny_z:
        copy.wait_recv()
    tiny_c = push(small_z.at[c], small_z.at[c], at(dc=1))
    arrived(3, 1, 6)
    arrived(7, 1, 0, 4, 6)
    enter(1, 3, 2, 4)
    times(3, 2, 4)
    arrived(5, 1, 6)
    enter(1, 4, 2, parts=(3,))
    arrived(4, 1, 0)
    arrived(5, 1, 0)
    enter(1, 4, 2, parts=(0, 1))
    arrived(4, 1, 4)
    arrived(5, 1, 4)
    enter(1, 4, 2, parts=(2,))
    times(4, 2, 1, (1,))
    send_sums(1)
    times(4, 2, 1, (0,))
    tiny_c.wait_recv()

    rows_z = [(r // 2, r % 2) for r in range(8)]
    one = jnp.concatenate([small_z[cc, zz, 0:8, :] for zz, cc in rows_z], 0)
    coll = jnp.concatenate([small_z[cc, zz, 8:16, :] for zz, cc in rows_z], 0)
    gr, gi = one[:, 0:64], one[:, 64:128]
    cr, ci = coll[:, 0:64], coll[:, 64:128]
    density = jnp.sum(gr * eye, 0, keepdims=True)
    hartree_col = jnp.sum(coup[...] * density, 1, keepdims=True)
    diag_col = hartree_col + jnp.sum(hr * eye, 1, keepdims=True)
    diag_row = jnp.sum(diag_col * eye, 0, keepdims=True)
    fr = off_r + diag_col * eye
    fi = off_i
    comm_r = dot(fr, gr) - dot(fi, gi) - dot(gr, fr) + dot(gi, fi)
    comm_i = dot(fr, gi) + dot(fi, gr) - dot(gr, fi) - dot(gi, fr)
    d1_r[...] = comm_i + cr + cr.T
    d1_i[...] = ci - ci.T - comm_r

    from_cols = jnp.zeros((1, 256), F32)
    lane_group = iota((1, 256), 1) // 64
    row64 = iota((64, 64), 0)
    table = coup[...] + diag_col + diag_row
    table_wide = dot(table, repeat)
    row_wide = iota((64, 256), 0)
    for k in range(COLS):
        picked = jnp.sum(
            jnp.where(row_wide == cb * COLS + k, table_wide, 0.0), 0, keepdims=True
        )
        from_cols = jnp.where(lane_group == k, picked, from_cols)
    table_t = coup_t + diag_col + diag_row
    for i in range(ROWS):
        from_rows = jnp.sum(
            jnp.where(iota((64, 64), 1) == rb * ROWS + i, table_t, 0.0), 1, keepdims=True
        )
        rows = slice(i * 64, i * 64 + 64)
        factor = from_rows - from_cols
        out_r[rows, :] += factor * g2i[rows, :]
        out_i[rows, :] -= factor * g2r[rows, :]

    for ch in range(2):
        for g in range(2):
            sums[ch, g].wait_recv()
            lanes = slice(g * 128, g * 128 + 128)
            for comp in range(2):
                for ip in range(2):
                    cut = slice(ip * 128, ip * 128 + 128)
                    even, odd = half_swap(
                        part[ch, g, comp, 0:64, cut] + part_in[ch, g, comp, 0:64, cut],
                        part[ch, g, comp, 64:128, cut] + part_in[ch, g, comp, 64:128, cut],
                        lower,
                    )
                    top = ch * 256 + ip * 128
                    for first, value in ((top, even), (top + 64, odd)):
                        if comp == 0:
                            out_i[first : first + 64, lanes] -= value
                        else:
                            out_r[first : first + 64, lanes] += value
    for copy in sent:
        copy.wait_send()


def finish(a, b, c, d, out_a, out_b, out_c, out_d):
    for src, dst in ((a, out_a), (b, out_b), (c, out_c), (d, out_d)):
        dst[...] = src[...]


def on_device(g2_re, g2_im, g1_re, g1_im, hop_re, hop_im, coupling):
    vmem = pl.BlockSpec(memory_space=pltpu.VMEM)
    smem = pl.BlockSpec(memory_space=pltpu.SMEM)
    count = 72
    shapes = (
        jax.ShapeDtypeStruct((512, 256), F32),
        jax.ShapeDtypeStruct((512, 256), F32),
        jax.ShapeDtypeStruct((64, 64), F32),
        jax.ShapeDtypeStruct((64, 64), F32),
    )
    parts = pl.pallas_call(
        kernel,
        out_shape=shapes,
        in_specs=[vmem] * 7 + [smem] * 2,
        out_specs=(vmem,) * 4,
        scratch_shapes=[
            pltpu.VMEM((8, 2, 8, 64, 256), F32),
            pltpu.VMEM((8, 2, 2, 256, 256), F32),
            pltpu.VMEM((2, 2, 128, 256), F32),
            pltpu.VMEM((8, 2, 1536, 256), BF16),
            pltpu.VMEM((8, 512, 1024), BF16),
            pltpu.VMEM((2, 4, 2, 128, 256), F32),
            pltpu.VMEM((2, 2, 2, 128, 256), F32),
            pltpu.VMEM((4, 16, 128), F32),
            pltpu.VMEM((4, 16, 128), F32),
            pltpu.VMEM((2, 4, 16, 128), F32),
            pltpu.VMEM((2, 64, 512), F32),
            pltpu.VMEM((2, 256, 256), F32),
            pltpu.VMEM((64, 256), F32),
            pltpu.SemaphoreType.DMA((count,)),
            pltpu.SemaphoreType.DMA((count,)),
        ],
        compiler_params=pltpu.CompilerParams(
            collective_id=0, has_side_effects=True, vmem_limit_bytes=56 * 2**20
        ),
    )(g2_re, g2_im, g1_re.T, g1_im.T, hop_re, hop_im, coupling, hop_re, hop_im)
    return pl.pallas_call(
        finish, out_shape=shapes, in_specs=[vmem] * 4, out_specs=(vmem,) * 4
    )(*parts)


def solution(mesh):
    pairs = P("prow", ("pcol", "orb"))
    return jax.shard_map(
        on_device,
        mesh=mesh,
        in_specs=(pairs, pairs, pairs, pairs, P(), P(), P()),
        out_specs=(pairs, pairs, P(), P()),
        check_vma=False,
    )
```

```python
import functools

import jax
import jax.numpy as jnp
from jax import lax
from jax.experimental import pallas as pl
from jax.experimental.pallas import tpu as pltpu
from jax.sharding import PartitionSpec as P

HIGH = lax.Precision.HIGHEST
MESH = pl.DeviceIdType.MESH
F32 = jnp.float32
BF16 = jnp.bfloat16

ORB = 64
ROWS = 8
COLS = 4


def dot(a, b):
    return jnp.dot(a, b, precision=HIGH, preferred_element_type=F32)


def mxu(a, b):
    return jnp.dot(a, b, preferred_element_type=F32)


def iota(shape, dim):
    return lax.broadcasted_iota(jnp.int32, shape, dim)


def split(value):
    high = value.astype(BF16)
    return high, (value - high.astype(F32)).astype(BF16)


def half_swap(first, second, lower):
    return (
        jnp.where(lower, first, pltpu.roll(second, 64, 1)),
        jnp.where(lower, pltpu.roll(first, 64, 1), second),
    )


def kernel(
    g2r,
    g2i,
    g1r,
    g1i,
    hop_r,
    hop_i,
    coup,
    hop_r_s,
    hop_i_s,
    out_r,
    out_i,
    d1_r,
    d1_i,
    right,
    left,
    left_send,
    stack,
    lsplit,
    part,
    part_in,
    small_y,
    small_x,
    small_z,
    field_rows,
    kron,
    wide,
    send,
    recv,
):
    prow, pcol, orb = (lax.axis_index(n) for n in ("prow", "pcol", "orb"))
    z, c = prow // 2, prow % 2
    x = pcol % 4
    y = (pcol // 4) * 2 + orb
    rb = prow

    def at(dx=0, dy=0, dz=0, dc=0):
        xx, yy, zz, cc = (x + dx) % 4, (y + dy) % 4, (z + dz) % 4, (c + dc) % 2
        return (zz * 2 + cc, (yy // 2) * 4 + xx, yy % 2)

    def col_block(xx, yy):
        return (yy // 2) * 8 + xx * 2 + yy % 2

    cb = col_block(x, y)
    ya = y + 1 - 2 * orb
    yb = (y + 3 + 2 * orb) % 4
    dev_a = (prow, (ya // 2) * 4 + x, ya % 2)
    dev_b = (prow, (yb // 2) * 4 + x, yb % 2)

    partners = [
        at(dc=1),
        at(dx=1),
        at(dx=3),
        at(dx=2),
        at(dy=1),
        at(dy=3),
        at(dy=2),
        at(dz=1),
        at(dz=3),
        at(dz=2),
    ]
    barrier = pltpu.get_barrier_semaphore()
    for device in partners:
        pl.semaphore_signal(barrier, inc=1, device_id=device, device_id_type=MESH)

    sent = []

    def push(src, dst, device):
        n = len(sent)
        copy = pltpu.make_async_remote_copy(
            src_ref=src,
            dst_ref=dst,
            send_sem=send.at[n],
            recv_sem=recv.at[n],
            device_id=device,
            device_id_type=MESH,
        )
        copy.start()
        sent.append(copy)
        return copy

    lower = iota((64, 128), 1) < 64
    for ch in range(2):
        for comp, g in ((0, g2r), (1, g2i)):
            for kt in range(2):
                lanes = slice(kt * 128, kt * 128 + 128)
                for ip in range(2):
                    top = ch * 256 + ip * 128
                    even, odd = half_swap(
                        g[top : top + 64, lanes], g[top + 64 : top + 128, lanes], lower
                    )
                    to = slice(ip * 128, ip * 128 + 128)
                    right[0, ch, 4 * kt + comp, :, to] = even
                    right[0, ch, 4 * kt + 2 + comp, :, to] = odd
    for comp in range(2):
        for k in range(4):
            left[rb, 0, comp, k * 64 : k * 64 + 64, :] = right[0, orb, 2 * k + comp]
            left_send[k // 2, comp, (k % 2) * 64 : (k % 2) * 64 + 64, :] = right[
                0, 1 - orb, 2 * k + comp
            ]

    pl.semaphore_wait(barrier, len(partners))

    got = {}

    whole = pl.ds(0, 256)
    sides = pl.ds(0, 128), pl.ds(128, 128)

    def go(to, start, ch, first, last, device, lanes=whole):
        cut = pl.ds(first, last - first)
        got[to, ch, first, lanes.start] = push(
            right.at[start, ch, cut, :, lanes], right.at[to, ch, cut, :, lanes], device
        )

    def arrived(slot, ch, *firsts, lanes=whole):
        for first in firsts:
            got[slot, ch, first, lanes.start].wait_recv()

    def own_y(ch, first, last):
        go(1, 0, ch, first, last, at(dy=2))

    def own_x(ch, first, last):
        go(6, 0, ch, first, last, at(dx=1))
        go(2, 0, ch, first, last, at(dx=3))

    own_y(0, 0, 4)
    own_x(0, 6, 8)
    own_x(0, 0, 6)
    pre = [
        push(left_send.at[0], left.at[rb, 1, :, 0:128, :], dev_a),
        push(left_send.at[1], left.at[rb, 1, :, 128:256, :], dev_b),
    ]
    z_first = {}
    for d, name in ((1, "m"), (3, "p")):
        z_first[name, 0] = push(left.at[rb, 0], left.at[rb, 0], at(dz=d))
    own_y(0, 4, 6)
    own_y(0, 6, 8)
    own_x(1, 6, 8)
    sib = {(0, 0): push(left.at[rb, 0], left.at[rb, 0], at(dc=1))}

    same = iota((64, 256), 0) == iota((64, 256), 1) % 64
    repeat = same.astype(F32)
    wide[...] = dot(coup[...], repeat)
    diag_r = jnp.concatenate(
        [jnp.sum(jnp.where(same, g2r[i * 64 : i * 64 + 64, :], 0.0), 0, keepdims=True) for i in range(ROWS)], 0
    )
    diag_i = jnp.concatenate(
        [jnp.sum(jnp.where(same, g2i[i * 64 : i * 64 + 64, :], 0.0), 0, keepdims=True) for i in range(ROWS)], 0
    )
    weight = wide[pl.ds(pl.multiple_of(rb * ROWS, ROWS), ROWS), :]
    place = iota((256, 128), 1) - COLS * cb
    group = iota((256, 128), 0) // 64
    to_re = (place == group).astype(F32)
    to_im = (place == group + 64).astype(F32)
    small_y[0, 8:16, :] = dot(weight * diag_i, to_re) - dot(weight * diag_r, to_im)
    spot = iota((8, 128), 1) - COLS * cb
    eye8 = iota((8, 8), 0) == iota((8, 8), 1)
    tile = jnp.zeros((8, 128), F32)
    for q in range(COLS):
        for lane, g1 in ((q, g1r), (q + 64, g1i)):
            column = jnp.sum(jnp.where(eye8, g1[q : q + 1, :], 0.0), 1, keepdims=True)
            tile = tile + jnp.where(spot == lane, column, 0.0)
    small_y[0, 0:8, :] = tile

    tiny_y = [
        push(small_y.at[0], small_y.at[n], at(dy=d)) for n, d in ((1, 1), (2, 3), (3, 2))
    ]

    eye = (iota((64, 64), 0) == iota((64, 64), 1)).astype(F32)
    hr, hi = hop_r[...], hop_i[...]
    off_r = 0.5 * (hr + hr.T) * (1.0 - eye)
    off_i = 0.5 * (hi - hi.T)
    choose = (iota((64, 512), 0) == rb * ROWS + iota((64, 512), 1) // 64).astype(F32)
    field_rows[0] = dot(off_r, choose)
    field_rows[1] = -dot(off_i, choose)
    block_diag = iota((256, 256), 0) // 64 == iota((256, 256), 1) // 64
    tall = (iota((256, 64), 0) % 64 == iota((256, 64), 1)).astype(F32)
    kron[0] = jnp.where(block_diag, dot(tall, dot(off_r, repeat)), 0.0)
    kron[1] = jnp.where(block_diag, dot(tall, dot(off_i, repeat)), 0.0)
    coup_t = coup[...].T

    def where_is(slot):
        return (x + slot // 2) % 4, (y + 2 * (slot % 2)) % 4

    for ch in range(2):
        for g in range(4):
            part[ch, g] = jnp.zeros((2, 128, 256), F32)

    def prepare(slot, ch, parts, lanes):
        base = col_block(*where_is(slot)) * COLS
        match = iota((64, lanes.size), 0) == iota((64, lanes.size), 1) % 64
        for a in parts:
            v = jnp.sum(
                jnp.where(iota((64, 64), 1) == base + a, coup_t, 0.0), 1, keepdims=True
            )
            for comp in range(2):
                value = v * right[slot, ch, 2 * a + comp, :, lanes] + jnp.where(
                    match,
                    field_rows[comp, pl.ds(base + a, 1), ch * 256 : ch * 256 + 256][
                        :, lanes.start : lanes.start + lanes.size
                    ],
                    0.0,
                )
                for n, term in enumerate(split(value)):
                    row = n * 768 + (1 - comp) * 256 + a * 64
                    stack[slot, ch, row : row + 64, lanes] = term
                    if comp == 1:
                        stack[slot, ch, row + 512 : row + 576, lanes] = -term

    def mix(slot, ch, parts, lanes):
        base = col_block(*where_is(slot)) * COLS
        starts = (cb * COLS, col_block(x, ya) * COLS, col_block(x, yb) * COLS)
        for kk in range(8):
            k = starts[0] + kk if kk < 4 else starts[1 if kk < 6 else 2] + kk - 4
            scale = {}
            for a in parts:
                sr = 0.5 * (hop_r_s[base + a, k] + hop_r_s[k, base + a])
                si = 0.5 * (hop_i_s[base + a, k] - hop_i_s[k, base + a])
                sr = jnp.where(k == base + a, 0.0, sr)
                scale[a] = tuple(jnp.full((8, lanes.size), f, F32) for f in (sr, si))
            for strip in range(8):
                to = slice((kk % 2) * 64 + strip * 8, (kk % 2) * 64 + strip * 8 + 8)
                rows = slice(strip * 8, strip * 8 + 8)
                acc_r = part[ch, kk // 2, 0, to, lanes]
                acc_i = part[ch, kk // 2, 1, to, lanes]
                for a in parts:
                    sr, si = scale[a]
                    tr = right[slot, ch, 2 * a, rows, lanes]
                    ti = right[slot, ch, 2 * a + 1, rows, lanes]
                    acc_r += si * ti - sr * tr
                    acc_i -= sr * ti + si * tr
                part[ch, kk // 2, 0, to, lanes] = acc_r
                part[ch, kk // 2, 1, to, lanes] = acc_i

    def enter(ch, first, count=1, stride=1, parts=(0, 1, 2, 3), lanes=whole):
        @pl.loop(0, count)
        def _(n):
            prepare(first + n * stride, ch, parts, lanes)
            mix(first + n * stride, ch, parts, lanes)

    def split_left(which, p):
        @pl.loop(0, 4)
        def _(step):
            rows = pl.ds(pl.multiple_of(step * 64, 64), 64)
            to = pl.ds(pl.multiple_of(p * 256 + step * 64, 64), 64)
            for comp in range(2):
                for n, term in enumerate(split(left[which, p, comp, rows, :])):
                    lane = n * 512 + comp * 256
                    lsplit[which, to, lane : lane + 256] = term

    def multiply(slot, ch, halves=(0, 1), lanes=whole):
        xx, yy = where_is(slot)
        which = (yy // 2) * 4 + xx
        rows = slice(halves[0] * 256, halves[-1] * 256 + 256)
        for comp in range(2):
            start = (1 - comp) * 256
            high = stack[slot, ch, start : start + 512, lanes]
            low = stack[slot, ch, start + 768 : start + 1280, lanes]
            value = (
                mxu(lsplit[which, rows, 0:512], high)
                + mxu(lsplit[which, rows, 0:512], low)
                + mxu(lsplit[which, rows, 512:1024], high)
            )
            for n in range(2 * len(halves)):
                part[ch, 2 * halves[0] + n, comp, :, lanes] += value[n * 128 : n * 128 + 128]

    def slot_of(zz, cc):
        return ((2 * (zz % 2) + cc - x + 4) % 4) * 2 + (zz // 2 + y // 2) % 2

    def along_x(ch, first):
        arrived(1, ch, first)
        go(7, 1, ch, first, 4 + first // 2, at(dx=1))
        go(3, 1, ch, first, 4 + first // 2, at(dx=3))

    def along_x_sides():
        arrived(1, 1, 0, 4)
        for lanes in sides:
            go(7, 1, 1, 0, 6, at(dx=1), lanes)
            go(3, 1, 1, 0, 6, at(dx=3), lanes)

    def relay_few_x(ch):
        arrived(6, ch, 6)
        arrived(2, ch, 6)
        go(4, 6, ch, 6, 7, at(dx=1))
        go(4, 2, ch, 7, 8, at(dx=3))

    def relay_few_y(ch):
        go(7, 6, ch, 6, 8, at(dy=2))
        go(3, 2, ch, 6, 8, at(dy=2))

    def relay(ch):
        arrived(6, ch, 0)
        if ch == 0:
            go(4, 6, 0, 0, 6, at(dx=1))
        else:
            go(4, 6, 1, 0, 6, at(dx=1), sides[0])
            go(4, 6, 1, 0, 4, at(dx=1), sides[1])
            go(4, 6, 1, 4, 6, at(dx=1), sides[1])
        arrived(2, ch, 0)

    def relay_far(ch):
        arrived(4, ch, 6, 7)
        go(5, 4, ch, 6, 8, at(dy=2))

    def relay_last(ch, first):
        arrived(3, ch, first)
        go(5, 3, ch, first, 4 + first // 2, at(dx=3))

    def relay_last_side(n):
        arrived(3, 1, 0, lanes=sides[n])
        for first, last in ((0, 6),) if n == 0 else ((0, 4), (4, 6)):
            go(5, 3, 1, first, last, at(dx=3), sides[n])

    rb_m = ((z + 3) % 4) * 2 + c
    rb_p = ((z + 1) % 4) * 2 + c
    rb_2 = ((z + 2) % 4) * 2 + c
    z_second = {}

    def pass_on(p):
        z_first["m", p].wait_recv()
        z_second[0, p] = push(left.at[rb_m, p, 0], left.at[rb_m, p, 0], at(dz=1))
        sib[3, p] = push(left.at[rb_m, p], left.at[rb_m, p], at(dc=1))
        z_first["p", p].wait_recv()
        z_second[1, p] = push(left.at[rb_p, p, 1], left.at[rb_p, p, 1], at(dz=3))
        sib[1, p] = push(left.at[rb_p, p], left.at[rb_p, p], at(dc=1))

    def pass_far(p):
        z_second[0, p].wait_recv()
        z_second[1, p].wait_recv()
        sib[2, p] = push(left.at[rb_2, p], left.at[rb_2, p], at(dc=1))
        split_left(rb_2, p)

    def from_sibling(dz):
        for p in range(2):
            sib[dz, p].wait_recv()
            split_left(((z + dz) % 4) * 2 + 1 - c, p)

    def by_left(first, count, far):
        @pl.loop(0, count)
        def _(n):
            slot = slot_of((z + 3 + (first + n) // 2) % 4, n % 2)

            @pl.when((slot // 2 == 2) == far)
            def _():
                multiply(slot, 0)

    def times(first, count, stride, halves=(0, 1), lanes=whole):
        @pl.loop(0, count)
        def _(n):
            multiply(first + n * stride, 1, halves, lanes)

    sums = {}

    def send_sums(ch, lanes=whole):
        for g, device in enumerate((dev_a, dev_b)):
            sums[ch, g, lanes.start] = push(
                part.at[ch, 2 + g, :, :, lanes], part_in.at[ch, g, :, :, lanes], device
            )

    relay_few_x(0)
    relay_few_y(0)
    enter(0, 0)
    along_x(0, 0)
    enter(1, 0)
    split_left(rb, 0)

    for half in range(2):
        rows = slice(half * 256, half * 256 + 256)
        gr, gi = g2r[rows, :], g2i[rows, :]
        kr, ki = kron[0], kron[1]
        out_r[rows, :] = dot(kr, gi) + dot(ki, gr) - dot(gr, ki) - dot(gi, kr)
        out_i[rows, :] = dot(ki, gi) - dot(kr, gr) + dot(gr, kr) - dot(gi, ki)

    for copy in pre:
        copy.wait_recv()
    for d, name in ((1, "m"), (3, "p")):
        z_first[name, 1] = push(left.at[rb, 1], left.at[rb, 1], at(dz=d))
    sib[0, 1] = push(left.at[rb, 1], left.at[rb, 1], at(dc=1))
    pass_on(0)
    split_left(rb, 1)
    along_x(0, 4)
    relay(0)
    relay_far(0)
    own_y(1, 0, 4)
    own_y(1, 4, 6)
    relay_few_x(1)
    relay_few_y(1)
    own_y(1, 6, 8)
    split_left(rb_m, 0)
    split_left(rb_p, 0)
    arrived(1, 0, 6)
    enter(0, 1)
    enter(0, 2, 2, 4)
    relay_last(0, 0)
    for copy in tiny_y:
        copy.wait_recv()
    small_x[0] = small_y[0] + small_y[1] + small_y[2] + small_y[3]
    tiny_x = [
        push(small_x.at[0], small_x.at[n], at(dx=d)) for n, d in ((1, 1), (2, 3), (3, 2))
    ]
    relay_last(0, 4)
    own_x(1, 0, 6)
    arrived(3, 0, 6)
    arrived(7, 0, 0, 4, 6)
    enter(0, 3, 2, 4)
    pass_on(1)
    from_sibling(0)
    split_left(rb_m, 1)
    split_left(rb_p, 1)
    from_sibling(3)
    from_sibling(1)
    by_left(0, 6, False)
    along_x_sides()
    relay_far(1)
    arrived(4, 0, 0)
    arrived(5, 0, 0, 4, 6)
    enter(0, 4, 2)
    by_left(0, 6, True)
    for copy in tiny_x:
        copy.wait_recv()
    small_z[c, z] = small_x[0] + small_x[1] + small_x[2] + small_x[3]
    tiny_z = [
        push(small_z.at[c, z], small_z.at[c, z], at(dz=d)) for d in (1, 3, 2)
    ]
    pass_far(0)
    pass_far(1)
    from_sibling(2)
    by_left(6, 2, False)
    by_left(6, 2, True)
    send_sums(0)
    relay(1)
    arrived(1, 1, 6)
    enter(1, 1)
    enter(1, 2, 2, 4)
    times(0, 2, 1)
    relay_last_side(0)
    times(2, 2, 4)
    relay_last_side(1)
    for copy in tiny_z:
        copy.wait_recv()
    tiny_c = push(small_z.at[c], small_z.at[c], at(dc=1))
    arrived(3, 1, 6)
    arrived(7, 1, 6)
    for lanes in sides:
        arrived(7, 1, 0, lanes=lanes)
    enter(1, 3, 2, 4)
    times(3, 2, 4)
    arrived(5, 1, 6)
    enter(1, 4, 2, parts=(3,))
    for slot in (4, 5):
        arrived(slot, 1, 0, lanes=sides[0])
    enter(1, 4, 2, 1, (0, 1, 2), sides[0])
    times(4, 2, 1, (1,), sides[0])
    send_sums(1, sides[0])
    for slot in (4, 5):
        arrived(slot, 1, 0, lanes=sides[1])
    enter(1, 4, 2, 1, (0, 1), sides[1])
    for slot in (4, 5):
        arrived(slot, 1, 4, lanes=sides[1])
    enter(1, 4, 2, 1, (2,), sides[1])
    times(4, 2, 1, (1,), sides[1])
    send_sums(1, sides[1])
    times(4, 2, 1, (0,))
    tiny_c.wait_recv()

    rows_z = [(r // 2, r % 2) for r in range(8)]
    one = jnp.concatenate([small_z[cc, zz, 0:8, :] for zz, cc in rows_z], 0)
    coll = jnp.concatenate([small_z[cc, zz, 8:16, :] for zz, cc in rows_z], 0)
    gr, gi = one[:, 0:64], one[:, 64:128]
    cr, ci = coll[:, 0:64], coll[:, 64:128]
    density = jnp.sum(gr * eye, 0, keepdims=True)
    hartree_col = jnp.sum(coup[...] * density, 1, keepdims=True)
    diag_col = hartree_col + jnp.sum(hr * eye, 1, keepdims=True)
    diag_row = jnp.sum(diag_col * eye, 0, keepdims=True)
    fr = off_r + diag_col * eye
    fi = off_i
    comm_r = dot(fr, gr) - dot(fi, gi) - dot(gr, fr) + dot(gi, fi)
    comm_i = dot(fr, gi) + dot(fi, gr) - dot(gr, fi) - dot(gi, fr)
    d1_r[...] = comm_i + cr + cr.T
    d1_i[...] = ci - ci.T - comm_r

    from_cols = jnp.zeros((1, 256), F32)
    lane_group = iota((1, 256), 1) // 64
    row64 = iota((64, 64), 0)
    table = coup[...] + diag_col + diag_row
    table_wide = dot(table, repeat)
    row_wide = iota((64, 256), 0)
    for k in range(COLS):
        picked = jnp.sum(
            jnp.where(row_wide == cb * COLS + k, table_wide, 0.0), 0, keepdims=True
        )
        from_cols = jnp.where(lane_group == k, picked, from_cols)
    table_t = coup_t + diag_col + diag_row
    for i in range(ROWS):
        from_rows = jnp.sum(
            jnp.where(iota((64, 64), 1) == rb * ROWS + i, table_t, 0.0), 1, keepdims=True
        )
        rows = slice(i * 64, i * 64 + 64)
        factor = from_rows - from_cols
        out_r[rows, :] += factor * g2i[rows, :]
        out_i[rows, :] -= factor * g2r[rows, :]

    for ch in range(2):
        for g in range(2):
            sums[ch, g, 0].wait_recv()
            if ch == 1:
                sums[1, g, 128].wait_recv()
            lanes = slice(g * 128, g * 128 + 128)
            for comp in range(2):
                for ip in range(2):
                    cut = slice(ip * 128, ip * 128 + 128)
                    even, odd = half_swap(
                        part[ch, g, comp, 0:64, cut] + part_in[ch, g, comp, 0:64, cut],
                        part[ch, g, comp, 64:128, cut] + part_in[ch, g, comp, 64:128, cut],
                        lower,
                    )
                    top = ch * 256 + ip * 128
                    for first, value in ((top, even), (top + 64, odd)):
                        if comp == 0:
                            out_i[first : first + 64, lanes] -= value
                        else:
                            out_r[first : first + 64, lanes] += value
    for copy in sent:
        copy.wait_send()


def finish(a, b, c, d, out_a, out_b, out_c, out_d):
    for src, dst in ((a, out_a), (b, out_b), (c, out_c), (d, out_d)):
        dst[...] = src[...]


def on_device(g2_re, g2_im, g1_re, g1_im, hop_re, hop_im, coupling):
    vmem = pl.BlockSpec(memory_space=pltpu.VMEM)
    smem = pl.BlockSpec(memory_space=pltpu.SMEM)
    count = 96
    shapes = (
        jax.ShapeDtypeStruct((512, 256), F32),
        jax.ShapeDtypeStruct((512, 256), F32),
        jax.ShapeDtypeStruct((64, 64), F32),
        jax.ShapeDtypeStruct((64, 64), F32),
    )
    parts = pl.pallas_call(
        kernel,
        out_shape=shapes,
        in_specs=[vmem] * 7 + [smem] * 2,
        out_specs=(vmem,) * 4,
        scratch_shapes=[
            pltpu.VMEM((8, 2, 8, 64, 256), F32),
            pltpu.VMEM((8, 2, 2, 256, 256), F32),
            pltpu.VMEM((2, 2, 128, 256), F32),
            pltpu.VMEM((8, 2, 1536, 256), BF16),
            pltpu.VMEM((8, 512, 1024), BF16),
            pltpu.VMEM((2, 4, 2, 128, 256), F32),
            pltpu.VMEM((2, 2, 2, 128, 256), F32),
            pltpu.VMEM((4, 16, 128), F32),
            pltpu.VMEM((4, 16, 128), F32),
            pltpu.VMEM((2, 4, 16, 128), F32),
            pltpu.VMEM((2, 64, 512), F32),
            pltpu.VMEM((2, 256, 256), F32),
            pltpu.VMEM((64, 256), F32),
            pltpu.SemaphoreType.DMA((count,)),
            pltpu.SemaphoreType.DMA((count,)),
        ],
        compiler_params=pltpu.CompilerParams(
            collective_id=0, has_side_effects=True, vmem_limit_bytes=56 * 2**20
        ),
    )(g2_re, g2_im, g1_re.T, g1_im.T, hop_re, hop_im, coupling, hop_re, hop_im)
    return pl.pallas_call(
        finish, out_shape=shapes, in_specs=[vmem] * 4, out_specs=(vmem,) * 4
    )(*parts)


def solution(mesh):
    pairs = P("prow", ("pcol", "orb"))
    return jax.shard_map(
        on_device,
        mesh=mesh,
        in_specs=(pairs, pairs, pairs, pairs, P(), P(), P()),
        out_specs=(pairs, pairs, P(), P()),
        check_vma=False,
    )
```

```python
import functools

import jax
import jax.numpy as jnp
from jax import lax
from jax.experimental import pallas as pl
from jax.experimental.pallas import tpu as pltpu
from jax.sharding import PartitionSpec as P

HIGH = lax.Precision.HIGHEST
MESH = pl.DeviceIdType.MESH
F32 = jnp.float32
BF16 = jnp.bfloat16

ORB = 64
ROWS = 8
COLS = 4


def dot(a, b):
    return jnp.dot(a, b, precision=HIGH, preferred_element_type=F32)


def mxu(a, b):
    return jnp.dot(a, b, preferred_element_type=F32)


def iota(shape, dim):
    return lax.broadcasted_iota(jnp.int32, shape, dim)


def split(value):
    high = value.astype(BF16)
    return high, (value - high.astype(F32)).astype(BF16)


def half_swap(first, second, lower):
    return (
        jnp.where(lower, first, pltpu.roll(second, 64, 1)),
        jnp.where(lower, pltpu.roll(first, 64, 1), second),
    )


def kernel(
    g2r,
    g2i,
    g1r,
    g1i,
    hop_r,
    hop_i,
    coup,
    hop_r_s,
    hop_i_s,
    out_r,
    out_i,
    d1_r,
    d1_i,
    right,
    left,
    left_send,
    stack,
    lsplit,
    part,
    part_in,
    small_y,
    small_x,
    small_z,
    field_rows,
    kron,
    wide,
    send,
    recv,
):
    prow, pcol, orb = (lax.axis_index(n) for n in ("prow", "pcol", "orb"))
    z, c = prow // 2, prow % 2
    x = pcol % 4
    y = (pcol // 4) * 2 + orb
    rb = prow

    def at(dx=0, dy=0, dz=0, dc=0):
        xx, yy, zz, cc = (x + dx) % 4, (y + dy) % 4, (z + dz) % 4, (c + dc) % 2
        return (zz * 2 + cc, (yy // 2) * 4 + xx, yy % 2)

    def col_block(xx, yy):
        return (yy // 2) * 8 + xx * 2 + yy % 2

    cb = col_block(x, y)
    ya = y + 1 - 2 * orb
    yb = (y + 3 + 2 * orb) % 4
    dev_a = (prow, (ya // 2) * 4 + x, ya % 2)
    dev_b = (prow, (yb // 2) * 4 + x, yb % 2)

    partners = [
        at(dc=1),
        at(dx=1),
        at(dx=3),
        at(dx=2),
        at(dy=1),
        at(dy=3),
        at(dy=2),
        at(dz=1),
        at(dz=3),
        at(dz=2),
    ]
    barrier = pltpu.get_barrier_semaphore()
    for device in partners:
        pl.semaphore_signal(barrier, inc=1, device_id=device, device_id_type=MESH)

    sent = []

    def push(src, dst, device):
        n = len(sent)
        copy = pltpu.make_async_remote_copy(
            src_ref=src,
            dst_ref=dst,
            send_sem=send.at[n],
            recv_sem=recv.at[n],
            device_id=device,
            device_id_type=MESH,
        )
        copy.start()
        sent.append(copy)
        return copy

    lower = iota((64, 128), 1) < 64
    for ch in range(2):
        for comp, g in ((0, g2r), (1, g2i)):
            for kt in range(2):
                lanes = slice(kt * 128, kt * 128 + 128)
                for ip in range(2):
                    top = ch * 256 + ip * 128
                    even, odd = half_swap(
                        g[top : top + 64, lanes], g[top + 64 : top + 128, lanes], lower
                    )
                    to = slice(ip * 128, ip * 128 + 128)
                    right[0, ch, 4 * kt + comp, :, to] = even
                    right[0, ch, 4 * kt + 2 + comp, :, to] = odd
    for comp in range(2):
        for k in range(4):
            left[rb, 0, comp, k * 64 : k * 64 + 64, :] = right[0, orb, 2 * k + comp]
            left_send[k // 2, comp, (k % 2) * 64 : (k % 2) * 64 + 64, :] = right[
                0, 1 - orb, 2 * k + comp
            ]

    pl.semaphore_wait(barrier, len(partners))

    got = {}

    whole = pl.ds(0, 256)
    sides = pl.ds(0, 128), pl.ds(128, 128)

    def go(to, start, ch, first, last, device, lanes=whole):
        cut = pl.ds(first, last - first)
        got[to, ch, first, lanes.start] = push(
            right.at[start, ch, cut, :, lanes], right.at[to, ch, cut, :, lanes], device
        )

    def arrived(slot, ch, *firsts, lanes=whole):
        for first in firsts:
            got[slot, ch, first, lanes.start].wait_recv()

    def own_y(ch, first, last):
        go(1, 0, ch, first, last, at(dy=2))

    def own_x(ch, first, last):
        go(6, 0, ch, first, last, at(dx=1))
        go(2, 0, ch, first, last, at(dx=3))

    own_y(0, 0, 4)
    own_x(0, 6, 8)
    own_x(0, 0, 6)
    pre = [
        push(left_send.at[0], left.at[rb, 1, :, 0:128, :], dev_a),
        push(left_send.at[1], left.at[rb, 1, :, 128:256, :], dev_b),
    ]
    z_first = {}
    for d, name in ((1, "m"), (3, "p")):
        z_first[name, 0] = push(left.at[rb, 0], left.at[rb, 0], at(dz=d))
    own_y(0, 4, 6)
    own_y(0, 6, 8)
    own_x(1, 6, 8)
    sib = {(0, 0): push(left.at[rb, 0], left.at[rb, 0], at(dc=1))}

    same = iota((64, 256), 0) == iota((64, 256), 1) % 64
    repeat = same.astype(F32)
    wide[...] = dot(coup[...], repeat)
    diag_r = jnp.concatenate(
        [jnp.sum(jnp.where(same, g2r[i * 64 : i * 64 + 64, :], 0.0), 0, keepdims=True) for i in range(ROWS)], 0
    )
    diag_i = jnp.concatenate(
        [jnp.sum(jnp.where(same, g2i[i * 64 : i * 64 + 64, :], 0.0), 0, keepdims=True) for i in range(ROWS)], 0
    )
    weight = wide[pl.ds(pl.multiple_of(rb * ROWS, ROWS), ROWS), :]
    place = iota((256, 128), 1) - COLS * cb
    group = iota((256, 128), 0) // 64
    to_re = (place == group).astype(F32)
    to_im = (place == group + 64).astype(F32)
    small_y[0, 8:16, :] = dot(weight * diag_i, to_re) - dot(weight * diag_r, to_im)
    spot = iota((8, 128), 1) - COLS * cb
    eye8 = iota((8, 8), 0) == iota((8, 8), 1)
    tile = jnp.zeros((8, 128), F32)
    for q in range(COLS):
        for lane, g1 in ((q, g1r), (q + 64, g1i)):
            column = jnp.sum(jnp.where(eye8, g1[q : q + 1, :], 0.0), 1, keepdims=True)
            tile = tile + jnp.where(spot == lane, column, 0.0)
    small_y[0, 0:8, :] = tile

    tiny_y = [
        push(small_y.at[0], small_y.at[n], at(dy=d)) for n, d in ((1, 1), (2, 3), (3, 2))
    ]

    eye = (iota((64, 64), 0) == iota((64, 64), 1)).astype(F32)
    hr, hi = hop_r[...], hop_i[...]
    off_r = 0.5 * (hr + hr.T) * (1.0 - eye)
    off_i = 0.5 * (hi - hi.T)
    choose = (iota((64, 512), 0) == rb * ROWS + iota((64, 512), 1) // 64).astype(F32)
    field_rows[0] = dot(off_r, choose)
    field_rows[1] = -dot(off_i, choose)
    block_diag = iota((256, 256), 0) // 64 == iota((256, 256), 1) // 64
    tall = (iota((256, 64), 0) % 64 == iota((256, 64), 1)).astype(F32)
    kron[0] = jnp.where(block_diag, dot(tall, dot(off_r, repeat)), 0.0)
    kron[1] = jnp.where(block_diag, dot(tall, dot(off_i, repeat)), 0.0)
    coup_t = coup[...].T

    def where_is(slot):
        return (x + slot // 2) % 4, (y + 2 * (slot % 2)) % 4

    for ch in range(2):
        for g in range(4):
            part[ch, g] = jnp.zeros((2, 128, 256), F32)

    def prepare(slot, ch, parts, lanes):
        base = col_block(*where_is(slot)) * COLS
        match = iota((64, lanes.size), 0) == iota((64, lanes.size), 1) % 64
        for a in parts:
            v = jnp.sum(
                jnp.where(iota((64, 64), 1) == base + a, coup_t, 0.0), 1, keepdims=True
            )
            for comp in range(2):
                value = v * right[slot, ch, 2 * a + comp, :, lanes] + jnp.where(
                    match,
                    field_rows[comp, pl.ds(base + a, 1), ch * 256 : ch * 256 + 256][
                        :, lanes.start : lanes.start + lanes.size
                    ],
                    0.0,
                )
                for n, term in enumerate(split(value)):
                    row = n * 768 + (1 - comp) * 256 + a * 64
                    stack[slot, ch, row : row + 64, lanes] = term
                    if comp == 1:
                        stack[slot, ch, row + 512 : row + 576, lanes] = -term

    def mix(slot, ch, parts, lanes):
        base = col_block(*where_is(slot)) * COLS
        starts = (cb * COLS, col_block(x, ya) * COLS, col_block(x, yb) * COLS)
        for kk in range(8):
            k = starts[0] + kk if kk < 4 else starts[1 if kk < 6 else 2] + kk - 4
            scale = {}
            for a in parts:
                sr = 0.5 * (hop_r_s[base + a, k] + hop_r_s[k, base + a])
                si = 0.5 * (hop_i_s[base + a, k] - hop_i_s[k, base + a])
                sr = jnp.where(k == base + a, 0.0, sr)
                scale[a] = tuple(jnp.full((8, lanes.size), f, F32) for f in (sr, si))
            for strip in range(8):
                to = slice((kk % 2) * 64 + strip * 8, (kk % 2) * 64 + strip * 8 + 8)
                rows = slice(strip * 8, strip * 8 + 8)
                acc_r = part[ch, kk // 2, 0, to, lanes]
                acc_i = part[ch, kk // 2, 1, to, lanes]
                for a in parts:
                    sr, si = scale[a]
                    tr = right[slot, ch, 2 * a, rows, lanes]
                    ti = right[slot, ch, 2 * a + 1, rows, lanes]
                    acc_r += si * ti - sr * tr
                    acc_i -= sr * ti + si * tr
                part[ch, kk // 2, 0, to, lanes] = acc_r
                part[ch, kk // 2, 1, to, lanes] = acc_i

    def enter(ch, first, count=1, stride=1, parts=(0, 1, 2, 3), lanes=whole):
        @pl.loop(0, count)
        def _(n):
            prepare(first + n * stride, ch, parts, lanes)
            mix(first + n * stride, ch, parts, lanes)

    def split_left(which, p):
        @pl.loop(0, 4)
        def _(step):
            rows = pl.ds(pl.multiple_of(step * 64, 64), 64)
            to = pl.ds(pl.multiple_of(p * 256 + step * 64, 64), 64)
            for comp in range(2):
                for n, term in enumerate(split(left[which, p, comp, rows, :])):
                    lane = n * 512 + comp * 256
                    lsplit[which, to, lane : lane + 256] = term

    def multiply(slot, ch, halves=(0, 1), lanes=whole):
        xx, yy = where_is(slot)
        which = (yy // 2) * 4 + xx
        rows = slice(halves[0] * 256, halves[-1] * 256 + 256)
        for comp in range(2):
            start = (1 - comp) * 256
            high = stack[slot, ch, start : start + 512, lanes]
            low = stack[slot, ch, start + 768 : start + 1280, lanes]
            value = (
                mxu(lsplit[which, rows, 0:512], high)
                + mxu(lsplit[which, rows, 0:512], low)
                + mxu(lsplit[which, rows, 512:1024], high)
            )
            for n in range(2 * len(halves)):
                part[ch, 2 * halves[0] + n, comp, :, lanes] += value[n * 128 : n * 128 + 128]

    def slot_of(zz, cc):
        return ((2 * (zz % 2) + cc - x + 4) % 4) * 2 + (zz // 2 + y // 2) % 2

    def along_x(ch, first):
        arrived(1, ch, first)
        go(7, 1, ch, first, 4 + first // 2, at(dx=1))
        go(3, 1, ch, first, 4 + first // 2, at(dx=3))

    def along_x_sides():
        arrived(1, 1, 0, 4)
        for lanes in sides:
            go(7, 1, 1, 0, 6, at(dx=1), lanes)
            go(3, 1, 1, 0, 6, at(dx=3), lanes)

    def relay_few_x(ch):
        arrived(6, ch, 6)
        arrived(2, ch, 6)
        go(4, 6, ch, 6, 7, at(dx=1))
        go(4, 2, ch, 7, 8, at(dx=3))

    def relay_few_y(ch):
        go(7, 6, ch, 6, 8, at(dy=2))
        go(3, 2, ch, 6, 8, at(dy=2))

    def relay(ch):
        arrived(6, ch, 0)
        if ch == 0:
            go(4, 6, 0, 0, 6, at(dx=1))
        else:
            go(4, 6, 1, 0, 6, at(dx=1), sides[0])
            go(4, 6, 1, 0, 4, at(dx=1), sides[1])
            go(4, 6, 1, 4, 6, at(dx=1), sides[1])
        arrived(2, ch, 0)

    def relay_far(ch):
        arrived(4, ch, 6, 7)
        go(5, 4, ch, 6, 8, at(dy=2))

    def relay_last(ch, first):
        arrived(3, ch, first)
        go(5, 3, ch, first, 4 + first // 2, at(dx=3))

    def relay_last_side(n):
        arrived(3, 1, 0, lanes=sides[n])
        for first, last in ((0, 6),) if n == 0 else ((0, 4), (4, 6)):
            go(5, 3, 1, first, last, at(dx=3), sides[n])

    rb_m = ((z + 3) % 4) * 2 + c
    rb_p = ((z + 1) % 4) * 2 + c
    rb_2 = ((z + 2) % 4) * 2 + c
    z_second = {}

    def pass_on(p):
        z_first["m", p].wait_recv()
        z_second[0, p] = push(left.at[rb_m, p, 0], left.at[rb_m, p, 0], at(dz=1))
        sib[3, p] = push(left.at[rb_m, p], left.at[rb_m, p], at(dc=1))
        z_first["p", p].wait_recv()
        z_second[1, p] = push(left.at[rb_p, p, 1], left.at[rb_p, p, 1], at(dz=3))
        sib[1, p] = push(left.at[rb_p, p], left.at[rb_p, p], at(dc=1))

    def pass_far(p):
        z_second[0, p].wait_recv()
        z_second[1, p].wait_recv()
        sib[2, p] = push(left.at[rb_2, p], left.at[rb_2, p], at(dc=1))
        split_left(rb_2, p)

    def from_sibling(dz):
        for p in range(2):
            sib[dz, p].wait_recv()
            split_left(((z + dz) % 4) * 2 + 1 - c, p)

    def by_left(first, count, far):
        @pl.loop(0, count)
        def _(n):
            slot = slot_of((z + 3 + (first + n) // 2) % 4, n % 2)

            @pl.when((slot // 2 == 2) == far)
            def _():
                multiply(slot, 0)

    def times(first, count, stride, halves=(0, 1), lanes=whole):
        @pl.loop(0, count)
        def _(n):
            multiply(first + n * stride, 1, halves, lanes)

    sums = {}

    def send_sums(ch, lanes=whole):
        for g, device in enumerate((dev_a, dev_b)):
            sums[ch, g, lanes.start] = push(
                part.at[ch, 2 + g, :, :, lanes], part_in.at[ch, g, :, :, lanes], device
            )

    relay_few_x(0)
    relay_few_y(0)
    enter(0, 0)
    along_x(0, 0)
    enter(1, 0)
    split_left(rb, 0)

    for half in range(2):
        rows = slice(half * 256, half * 256 + 256)
        gr, gi = g2r[rows, :], g2i[rows, :]
        kr, ki = kron[0], kron[1]
        out_r[rows, :] = dot(kr, gi) + dot(ki, gr) - dot(gr, ki) - dot(gi, kr)
        out_i[rows, :] = dot(ki, gi) - dot(kr, gr) + dot(gr, kr) - dot(gi, ki)

    for copy in pre:
        copy.wait_recv()
    for d, name in ((1, "m"), (3, "p")):
        z_first[name, 1] = push(left.at[rb, 1], left.at[rb, 1], at(dz=d))
    sib[0, 1] = push(left.at[rb, 1], left.at[rb, 1], at(dc=1))
    pass_on(0)
    split_left(rb, 1)
    along_x(0, 4)
    relay(0)
    relay_far(0)
    own_y(1, 0, 4)
    own_y(1, 4, 6)
    relay_few_x(1)
    relay_few_y(1)
    own_y(1, 6, 8)
    split_left(rb_m, 0)
    split_left(rb_p, 0)
    arrived(1, 0, 6)
    enter(0, 1)
    enter(0, 2, 2, 4)
    relay_last(0, 0)
    for copy in tiny_y:
        copy.wait_recv()
    small_x[0] = small_y[0] + small_y[1] + small_y[2] + small_y[3]
    tiny_x = [
        push(small_x.at[0], small_x.at[n], at(dx=d)) for n, d in ((1, 1), (2, 3), (3, 2))
    ]
    relay_last(0, 4)
    own_x(1, 0, 6)
    arrived(3, 0, 6)
    arrived(7, 0, 0, 4, 6)
    enter(0, 3, 2, 4)
    pass_on(1)
    from_sibling(0)
    split_left(rb_m, 1)
    split_left(rb_p, 1)
    by_left(2, 2, False)
    from_sibling(3)
    by_left(0, 2, False)
    from_sibling(1)
    by_left(4, 2, False)
    along_x_sides()
    relay_far(1)
    arrived(4, 0, 0)
    arrived(5, 0, 0, 4, 6)
    enter(0, 4, 2)
    by_left(0, 6, True)
    for copy in tiny_x:
        copy.wait_recv()
    small_z[c, z] = small_x[0] + small_x[1] + small_x[2] + small_x[3]
    tiny_z = [
        push(small_z.at[c, z], small_z.at[c, z], at(dz=d)) for d in (1, 3, 2)
    ]
    pass_far(0)
    pass_far(1)
    enter(1, 1, parts=(0, 1, 2))
    from_sibling(2)
    by_left(6, 2, False)
    by_left(6, 2, True)
    send_sums(0)
    relay(1)
    arrived(1, 1, 6)
    enter(1, 1, parts=(3,))
    enter(1, 2, 2, 4)
    times(0, 2, 1)
    relay_last_side(0)
    times(2, 2, 4)
    relay_last_side(1)
    for copy in tiny_z:
        copy.wait_recv()
    tiny_c = push(small_z.at[c], small_z.at[c], at(dc=1))
    arrived(3, 1, 6)
    arrived(7, 1, 6)
    for lanes in sides:
        arrived(7, 1, 0, lanes=lanes)
    enter(1, 3, 2, 4)
    times(3, 2, 4)
    arrived(5, 1, 6)
    enter(1, 4, 2, parts=(3,))
    for slot in (4, 5):
        arrived(slot, 1, 0, lanes=sides[0])
    enter(1, 4, 2, 1, (0, 1, 2), sides[0])
    times(4, 2, 1, (1,), sides[0])
    send_sums(1, sides[0])
    for slot in (4, 5):
        arrived(slot, 1, 0, lanes=sides[1])
    enter(1, 4, 2, 1, (0, 1), sides[1])
    for slot in (4, 5):
        arrived(slot, 1, 4, lanes=sides[1])
    enter(1, 4, 2, 1, (2,), sides[1])
    times(4, 2, 1, (1,), sides[1])
    send_sums(1, sides[1])
    times(4, 2, 1, (0,))
    tiny_c.wait_recv()

    rows_z = [(r // 2, r % 2) for r in range(8)]
    one = jnp.concatenate([small_z[cc, zz, 0:8, :] for zz, cc in rows_z], 0)
    coll = jnp.concatenate([small_z[cc, zz, 8:16, :] for zz, cc in rows_z], 0)
    gr, gi = one[:, 0:64], one[:, 64:128]
    cr, ci = coll[:, 0:64], coll[:, 64:128]
    density = jnp.sum(gr * eye, 0, keepdims=True)
    hartree_col = jnp.sum(coup[...] * density, 1, keepdims=True)
    diag_col = hartree_col + jnp.sum(hr * eye, 1, keepdims=True)
    diag_row = jnp.sum(diag_col * eye, 0, keepdims=True)
    fr = off_r + diag_col * eye
    fi = off_i
    comm_r = dot(fr, gr) - dot(fi, gi) - dot(gr, fr) + dot(gi, fi)
    comm_i = dot(fr, gi) + dot(fi, gr) - dot(gr, fi) - dot(gi, fr)
    d1_r[...] = comm_i + cr + cr.T
    d1_i[...] = ci - ci.T - comm_r

    from_cols = jnp.zeros((1, 256), F32)
    lane_group = iota((1, 256), 1) // 64
    row64 = iota((64, 64), 0)
    table = coup[...] + diag_col + diag_row
    table_wide = dot(table, repeat)
    row_wide = iota((64, 256), 0)
    for k in range(COLS):
        picked = jnp.sum(
            jnp.where(row_wide == cb * COLS + k, table_wide, 0.0), 0, keepdims=True
        )
        from_cols = jnp.where(lane_group == k, picked, from_cols)
    table_t = coup_t + diag_col + diag_row
    for i in range(ROWS):
        from_rows = jnp.sum(
            jnp.where(iota((64, 64), 1) == rb * ROWS + i, table_t, 0.0), 1, keepdims=True
        )
        rows = slice(i * 64, i * 64 + 64)
        factor = from_rows - from_cols
        out_r[rows, :] += factor * g2i[rows, :]
        out_i[rows, :] -= factor * g2r[rows, :]

    for ch in range(2):
        for g in range(2):
            sums[ch, g, 0].wait_recv()
            if ch == 1:
                sums[1, g, 128].wait_recv()
            lanes = slice(g * 128, g * 128 + 128)
            for comp in range(2):
                for ip in range(2):
                    cut = slice(ip * 128, ip * 128 + 128)
                    even, odd = half_swap(
                        part[ch, g, comp, 0:64, cut] + part_in[ch, g, comp, 0:64, cut],
                        part[ch, g, comp, 64:128, cut] + part_in[ch, g, comp, 64:128, cut],
                        lower,
                    )
                    top = ch * 256 + ip * 128
                    for first, value in ((top, even), (top + 64, odd)):
                        if comp == 0:
                            out_i[first : first + 64, lanes] -= value
                        else:
                            out_r[first : first + 64, lanes] += value
    for copy in sent:
        copy.wait_send()


def finish(a, b, c, d, out_a, out_b, out_c, out_d, done):
    pairs = ((a, out_a), (b, out_b), (c, out_c), (d, out_d))
    copies = [pltpu.make_async_copy(*pair, done.at[n]) for n, pair in enumerate(pairs)]
    for copy in copies:
        copy.start()
    for copy in copies:
        copy.wait()


def on_device(g2_re, g2_im, g1_re, g1_im, hop_re, hop_im, coupling):
    vmem = pl.BlockSpec(memory_space=pltpu.VMEM)
    smem = pl.BlockSpec(memory_space=pltpu.SMEM)
    anywhere = pl.BlockSpec(memory_space=pl.ANY)
    count = 96
    shapes = (
        jax.ShapeDtypeStruct((512, 256), F32),
        jax.ShapeDtypeStruct((512, 256), F32),
        jax.ShapeDtypeStruct((64, 64), F32),
        jax.ShapeDtypeStruct((64, 64), F32),
    )
    parts = pl.pallas_call(
        kernel,
        out_shape=shapes,
        in_specs=[vmem] * 7 + [smem] * 2,
        out_specs=(vmem,) * 4,
        scratch_shapes=[
            pltpu.VMEM((8, 2, 8, 64, 256), F32),
            pltpu.VMEM((8, 2, 2, 256, 256), F32),
            pltpu.VMEM((2, 2, 128, 256), F32),
            pltpu.VMEM((8, 2, 1536, 256), BF16),
            pltpu.VMEM((8, 512, 1024), BF16),
            pltpu.VMEM((2, 4, 2, 128, 256), F32),
            pltpu.VMEM((2, 2, 2, 128, 256), F32),
            pltpu.VMEM((4, 16, 128), F32),
            pltpu.VMEM((4, 16, 128), F32),
            pltpu.VMEM((2, 4, 16, 128), F32),
            pltpu.VMEM((2, 64, 512), F32),
            pltpu.VMEM((2, 256, 256), F32),
            pltpu.VMEM((64, 256), F32),
            pltpu.SemaphoreType.DMA((count,)),
            pltpu.SemaphoreType.DMA((count,)),
        ],
        compiler_params=pltpu.CompilerParams(
            collective_id=0, has_side_effects=True, vmem_limit_bytes=56 * 2**20
        ),
    )(g2_re, g2_im, g1_re.T, g1_im.T, hop_re, hop_im, coupling, hop_re, hop_im)
    return pl.pallas_call(
        finish,
        out_shape=shapes,
        in_specs=[anywhere] * 4,
        out_specs=(anywhere,) * 4,
        scratch_shapes=[pltpu.SemaphoreType.DMA((4,))],
    )(*parts)


def solution(mesh):
    pairs = P("prow", ("pcol", "orb"))
    return jax.shard_map(
        on_device,
        mesh=mesh,
        in_specs=(pairs, pairs, pairs, pairs, P(), P(), P()),
        out_specs=(pairs, pairs, P(), P()),
        check_vma=False,
    )
```

```python
import functools

import jax
import jax.numpy as jnp
from jax import lax
from jax.experimental import pallas as pl
from jax.experimental.pallas import tpu as pltpu
from jax.sharding import PartitionSpec as P

HIGH = lax.Precision.HIGHEST
MESH = pl.DeviceIdType.MESH
F32 = jnp.float32
BF16 = jnp.bfloat16

ORB = 64
ROWS = 8
COLS = 4


def dot(a, b):
    return jnp.dot(a, b, precision=HIGH, preferred_element_type=F32)


def mxu(a, b):
    return jnp.dot(a, b, preferred_element_type=F32)


def iota(shape, dim):
    return lax.broadcasted_iota(jnp.int32, shape, dim)


def split(value):
    high = value.astype(BF16)
    return high, (value - high.astype(F32)).astype(BF16)


def half_swap(first, second, lower):
    return (
        jnp.where(lower, first, pltpu.roll(second, 64, 1)),
        jnp.where(lower, pltpu.roll(first, 64, 1), second),
    )


def kernel(
    g2r,
    g2i,
    g1r,
    g1i,
    hop_r,
    hop_i,
    coup,
    hop_r_s,
    hop_i_s,
    out_r,
    out_i,
    d1_r,
    d1_i,
    right,
    left,
    left_send,
    stack,
    lsplit,
    part,
    part_in,
    small_y,
    small_x,
    small_z,
    field_rows,
    kron,
    wide,
    send,
    recv,
):
    prow, pcol, orb = (lax.axis_index(n) for n in ("prow", "pcol", "orb"))
    z, c = prow // 2, prow % 2
    x = pcol % 4
    y = (pcol // 4) * 2 + orb
    rb = prow

    def at(dx=0, dy=0, dz=0, dc=0):
        xx, yy, zz, cc = (x + dx) % 4, (y + dy) % 4, (z + dz) % 4, (c + dc) % 2
        return (zz * 2 + cc, (yy // 2) * 4 + xx, yy % 2)

    def col_block(xx, yy):
        return (yy // 2) * 8 + xx * 2 + yy % 2

    cb = col_block(x, y)
    ya = y + 1 - 2 * orb
    yb = (y + 3 + 2 * orb) % 4
    dev_a = (prow, (ya // 2) * 4 + x, ya % 2)
    dev_b = (prow, (yb // 2) * 4 + x, yb % 2)

    partners = [
        at(dc=1),
        at(dx=1),
        at(dx=3),
        at(dx=2),
        at(dy=1),
        at(dy=3),
        at(dy=2),
        at(dz=1),
        at(dz=3),
        at(dz=2),
    ]
    barrier = pltpu.get_barrier_semaphore()
    for device in partners:
        pl.semaphore_signal(barrier, inc=1, device_id=device, device_id_type=MESH)

    sent = []

    def push(src, dst, device):
        n = len(sent)
        copy = pltpu.make_async_remote_copy(
            src_ref=src,
            dst_ref=dst,
            send_sem=send.at[n],
            recv_sem=recv.at[n],
            device_id=device,
            device_id_type=MESH,
        )
        copy.start()
        sent.append(copy)
        return copy

    lower = iota((64, 128), 1) < 64
    for ch in range(2):
        for comp, g in ((0, g2r), (1, g2i)):
            for kt in range(2):
                lanes = slice(kt * 128, kt * 128 + 128)
                for ip in range(2):
                    top = ch * 256 + ip * 128
                    even, odd = half_swap(
                        g[top : top + 64, lanes], g[top + 64 : top + 128, lanes], lower
                    )
                    to = slice(ip * 128, ip * 128 + 128)
                    right[0, ch, 4 * kt + comp, :, to] = even
                    right[0, ch, 4 * kt + 2 + comp, :, to] = odd
    for comp in range(2):
        for k in range(4):
            left[rb, 0, comp, k * 64 : k * 64 + 64, :] = right[0, orb, 2 * k + comp]
            left_send[k // 2, comp, (k % 2) * 64 : (k % 2) * 64 + 64, :] = right[
                0, 1 - orb, 2 * k + comp
            ]

    pl.semaphore_wait(barrier, len(partners))

    got = {}

    whole = pl.ds(0, 256)
    sides = pl.ds(0, 128), pl.ds(128, 128)

    def go(to, start, ch, first, last, device, lanes=whole):
        cut = pl.ds(first, last - first)
        got[to, ch, first, lanes.start] = push(
            right.at[start, ch, cut, :, lanes], right.at[to, ch, cut, :, lanes], device
        )

    def arrived(slot, ch, *firsts, lanes=whole):
        for first in firsts:
            got[slot, ch, first, lanes.start].wait_recv()

    def own_y(ch, first, last):
        go(1, 0, ch, first, last, at(dy=2))

    def own_x(ch, first, last):
        go(6, 0, ch, first, last, at(dx=1))
        go(2, 0, ch, first, last, at(dx=3))

    own_y(0, 0, 4)
    own_x(0, 6, 8)
    own_x(0, 0, 6)
    pre = [
        push(left_send.at[0], left.at[rb, 1, :, 0:128, :], dev_a),
        push(left_send.at[1], left.at[rb, 1, :, 128:256, :], dev_b),
    ]
    z_first = {}
    for d, name in ((1, "m"), (3, "p")):
        z_first[name, 0] = push(left.at[rb, 0], left.at[rb, 0], at(dz=d))
    own_y(0, 4, 6)
    own_y(0, 6, 8)
    own_x(1, 6, 8)
    sib = {(0, 0): push(left.at[rb, 0], left.at[rb, 0], at(dc=1))}

    same = iota((64, 256), 0) == iota((64, 256), 1) % 64
    repeat = same.astype(F32)
    wide[...] = dot(coup[...], repeat)
    diag_r = jnp.concatenate(
        [jnp.sum(jnp.where(same, g2r[i * 64 : i * 64 + 64, :], 0.0), 0, keepdims=True) for i in range(ROWS)], 0
    )
    diag_i = jnp.concatenate(
        [jnp.sum(jnp.where(same, g2i[i * 64 : i * 64 + 64, :], 0.0), 0, keepdims=True) for i in range(ROWS)], 0
    )
    weight = wide[pl.ds(pl.multiple_of(rb * ROWS, ROWS), ROWS), :]
    place = iota((256, 128), 1) - COLS * cb
    group = iota((256, 128), 0) // 64
    to_re = (place == group).astype(F32)
    to_im = (place == group + 64).astype(F32)
    small_y[0, 8:16, :] = dot(weight * diag_i, to_re) - dot(weight * diag_r, to_im)
    spot = iota((8, 128), 1) - COLS * cb
    eye8 = iota((8, 8), 0) == iota((8, 8), 1)
    tile = jnp.zeros((8, 128), F32)
    for q in range(COLS):
        for lane, g1 in ((q, g1r), (q + 64, g1i)):
            column = jnp.sum(jnp.where(eye8, g1[q : q + 1, :], 0.0), 1, keepdims=True)
            tile = tile + jnp.where(spot == lane, column, 0.0)
    small_y[0, 0:8, :] = tile

    tiny_y = [
        push(small_y.at[0], small_y.at[n], at(dy=d)) for n, d in ((1, 1), (2, 3), (3, 2))
    ]

    eye = (iota((64, 64), 0) == iota((64, 64), 1)).astype(F32)
    hr, hi = hop_r[...], hop_i[...]
    off_r = 0.5 * (hr + hr.T) * (1.0 - eye)
    off_i = 0.5 * (hi - hi.T)
    choose = (iota((64, 512), 0) == rb * ROWS + iota((64, 512), 1) // 64).astype(F32)
    field_rows[0] = dot(off_r, choose)
    field_rows[1] = -dot(off_i, choose)
    block_diag = iota((256, 256), 0) // 64 == iota((256, 256), 1) // 64
    tall = (iota((256, 64), 0) % 64 == iota((256, 64), 1)).astype(F32)
    kron[0] = jnp.where(block_diag, dot(tall, dot(off_r, repeat)), 0.0)
    kron[1] = jnp.where(block_diag, dot(tall, dot(off_i, repeat)), 0.0)
    coup_t = coup[...].T

    def where_is(slot):
        return (x + slot // 2) % 4, (y + 2 * (slot % 2)) % 4

    for ch in range(2):
        for g in range(4):
            part[ch, g] = jnp.zeros((2, 128, 256), F32)

    def prepare(slot, ch, parts, lanes):
        base = col_block(*where_is(slot)) * COLS
        match = iota((64, lanes.size), 0) == iota((64, lanes.size), 1) % 64
        for a in parts:
            v = jnp.sum(
                jnp.where(iota((64, 64), 1) == base + a, coup_t, 0.0), 1, keepdims=True
            )
            for comp in range(2):
                value = v * right[slot, ch, 2 * a + comp, :, lanes] + jnp.where(
                    match,
                    field_rows[comp, pl.ds(base + a, 1), ch * 256 : ch * 256 + 256][
                        :, lanes.start : lanes.start + lanes.size
                    ],
                    0.0,
                )
                for n, term in enumerate(split(value)):
                    row = n * 768 + (1 - comp) * 256 + a * 64
                    stack[slot, ch, row : row + 64, lanes] = term
                    if comp == 1:
                        stack[slot, ch, row + 512 : row + 576, lanes] = -term

    def mix(slot, ch, parts, lanes):
        base = col_block(*where_is(slot)) * COLS
        starts = (cb * COLS, col_block(x, ya) * COLS, col_block(x, yb) * COLS)
        for kk in range(8):
            k = starts[0] + kk if kk < 4 else starts[1 if kk < 6 else 2] + kk - 4
            scale = {}
            for a in parts:
                sr = 0.5 * (hop_r_s[base + a, k] + hop_r_s[k, base + a])
                si = 0.5 * (hop_i_s[base + a, k] - hop_i_s[k, base + a])
                sr = jnp.where(k == base + a, 0.0, sr)
                scale[a] = tuple(jnp.full((8, lanes.size), f, F32) for f in (sr, si))
            for strip in range(8):
                to = slice((kk % 2) * 64 + strip * 8, (kk % 2) * 64 + strip * 8 + 8)
                rows = slice(strip * 8, strip * 8 + 8)
                acc_r = part[ch, kk // 2, 0, to, lanes]
                acc_i = part[ch, kk // 2, 1, to, lanes]
                for a in parts:
                    sr, si = scale[a]
                    tr = right[slot, ch, 2 * a, rows, lanes]
                    ti = right[slot, ch, 2 * a + 1, rows, lanes]
                    acc_r += si * ti - sr * tr
                    acc_i -= sr * ti + si * tr
                part[ch, kk // 2, 0, to, lanes] = acc_r
                part[ch, kk // 2, 1, to, lanes] = acc_i

    def enter(ch, first, count=1, stride=1, parts=(0, 1, 2, 3), lanes=whole):
        @pl.loop(0, count)
        def _(n):
            prepare(first + n * stride, ch, parts, lanes)
            mix(first + n * stride, ch, parts, lanes)

    def split_left(which, p):
        @pl.loop(0, 4)
        def _(step):
            rows = pl.ds(pl.multiple_of(step * 64, 64), 64)
            to = pl.ds(pl.multiple_of(p * 256 + step * 64, 64), 64)
            for comp in range(2):
                for n, term in enumerate(split(left[which, p, comp, rows, :])):
                    lane = n * 512 + comp * 256
                    lsplit[which, to, lane : lane + 256] = term

    def multiply(slot, ch, halves=(0, 1), lanes=whole):
        xx, yy = where_is(slot)
        which = (yy // 2) * 4 + xx
        rows = slice(halves[0] * 256, halves[-1] * 256 + 256)
        for comp in range(2):
            start = (1 - comp) * 256
            high = stack[slot, ch, start : start + 512, lanes]
            low = stack[slot, ch, start + 768 : start + 1280, lanes]
            value = (
                mxu(lsplit[which, rows, 0:512], high)
                + mxu(lsplit[which, rows, 0:512], low)
                + mxu(lsplit[which, rows, 512:1024], high)
            )
            for n in range(2 * len(halves)):
                part[ch, 2 * halves[0] + n, comp, :, lanes] += value[n * 128 : n * 128 + 128]

    def slot_of(zz, cc):
        return ((2 * (zz % 2) + cc - x + 4) % 4) * 2 + (zz // 2 + y // 2) % 2

    def along_x(ch, first):
        arrived(1, ch, first)
        go(7, 1, ch, first, 4 + first // 2, at(dx=1))
        go(3, 1, ch, first, 4 + first // 2, at(dx=3))

    def along_x_sides():
        arrived(1, 1, 0, 4)
        for lanes in sides:
            go(7, 1, 1, 0, 6, at(dx=1), lanes)
            go(3, 1, 1, 0, 6, at(dx=3), lanes)

    def relay_few_x(ch):
        arrived(6, ch, 6)
        arrived(2, ch, 6)
        go(4, 6, ch, 6, 7, at(dx=1))
        go(4, 2, ch, 7, 8, at(dx=3))

    def relay_few_y(ch):
        go(7, 6, ch, 6, 8, at(dy=2))
        go(3, 2, ch, 6, 8, at(dy=2))

    def relay(ch):
        arrived(6, ch, 0)
        if ch == 0:
            go(4, 6, 0, 0, 6, at(dx=1))
        else:
            go(4, 6, 1, 0, 6, at(dx=1), sides[0])
            go(4, 6, 1, 0, 4, at(dx=1), sides[1])
            go(4, 6, 1, 4, 6, at(dx=1), sides[1])
        arrived(2, ch, 0)

    def relay_far(ch):
        arrived(4, ch, 6, 7)
        go(5, 4, ch, 6, 8, at(dy=2))

    def relay_last(ch, first):
        arrived(3, ch, first)
        go(5, 3, ch, first, 4 + first // 2, at(dx=3))

    def relay_last_side(n):
        arrived(3, 1, 0, lanes=sides[n])
        for first, last in ((0, 6),) if n == 0 else ((0, 4), (4, 6)):
            go(5, 3, 1, first, last, at(dx=3), sides[n])

    rb_m = ((z + 3) % 4) * 2 + c
    rb_p = ((z + 1) % 4) * 2 + c
    rb_2 = ((z + 2) % 4) * 2 + c
    z_second = {}

    def pass_on(p):
        z_first["m", p].wait_recv()
        z_second[0, p] = push(left.at[rb_m, p, 0], left.at[rb_m, p, 0], at(dz=1))
        sib[3, p] = push(left.at[rb_m, p], left.at[rb_m, p], at(dc=1))
        z_first["p", p].wait_recv()
        z_second[1, p] = push(left.at[rb_p, p, 1], left.at[rb_p, p, 1], at(dz=3))
        sib[1, p] = push(left.at[rb_p, p], left.at[rb_p, p], at(dc=1))

    def pass_far(p):
        z_second[0, p].wait_recv()
        z_second[1, p].wait_recv()
        sib[2, p] = push(left.at[rb_2, p], left.at[rb_2, p], at(dc=1))
        split_left(rb_2, p)

    def from_sibling(dz):
        for p in range(2):
            sib[dz, p].wait_recv()
            split_left(((z + dz) % 4) * 2 + 1 - c, p)

    def by_left(first, count, far):
        @pl.loop(0, count)
        def _(n):
            slot = slot_of((z + 3 + (first + n) // 2) % 4, n % 2)

            @pl.when((slot // 2 == 2) == far)
            def _():
                multiply(slot, 0)

    def times(first, count, stride, halves=(0, 1), lanes=whole):
        @pl.loop(0, count)
        def _(n):
            multiply(first + n * stride, 1, halves, lanes)

    sums = {}

    def send_sums(ch, lanes=whole):
        for g, device in enumerate((dev_a, dev_b)):
            sums[ch, g, lanes.start] = push(
                part.at[ch, 2 + g, :, :, lanes], part_in.at[ch, g, :, :, lanes], device
            )

    relay_few_x(0)
    relay_few_y(0)
    enter(0, 0)
    along_x(0, 0)
    enter(1, 0)
    split_left(rb, 0)

    for half in range(2):
        rows = slice(half * 256, half * 256 + 256)
        gr, gi = g2r[rows, :], g2i[rows, :]
        kr, ki = kron[0], kron[1]
        out_r[rows, :] = dot(kr, gi) + dot(ki, gr) - dot(gr, ki) - dot(gi, kr)
        out_i[rows, :] = dot(ki, gi) - dot(kr, gr) + dot(gr, kr) - dot(gi, ki)

    for copy in pre:
        copy.wait_recv()
    for d, name in ((1, "m"), (3, "p")):
        z_first[name, 1] = push(left.at[rb, 1], left.at[rb, 1], at(dz=d))
    sib[0, 1] = push(left.at[rb, 1], left.at[rb, 1], at(dc=1))
    pass_on(0)
    split_left(rb, 1)
    along_x(0, 4)
    relay(0)
    relay_far(0)
    own_y(1, 0, 4)
    own_y(1, 4, 6)
    relay_few_x(1)
    relay_few_y(1)
    own_y(1, 6, 8)
    split_left(rb_m, 0)
    split_left(rb_p, 0)
    arrived(1, 0, 6)
    enter(0, 1)
    enter(0, 2, 2, 4)
    relay_last(0, 0)
    for copy in tiny_y:
        copy.wait_recv()
    small_x[0] = small_y[0] + small_y[1] + small_y[2] + small_y[3]
    tiny_x = [
        push(small_x.at[0], small_x.at[n], at(dx=d)) for n, d in ((1, 1), (2, 3), (3, 2))
    ]
    relay_last(0, 4)
    own_x(1, 0, 6)
    arrived(3, 0, 6)
    arrived(7, 0, 0, 4, 6)
    enter(0, 3, 2, 4)
    pass_on(1)
    from_sibling(0)
    split_left(rb_m, 1)
    split_left(rb_p, 1)
    by_left(2, 2, False)
    from_sibling(3)
    by_left(0, 2, False)
    from_sibling(1)
    by_left(4, 2, False)
    along_x_sides()
    relay_far(1)
    arrived(4, 0, 0)
    arrived(5, 0, 0, 4, 6)
    enter(0, 4, 2)
    by_left(0, 6, True)
    for copy in tiny_x:
        copy.wait_recv()
    small_z[c, z] = small_x[0] + small_x[1] + small_x[2] + small_x[3]
    tiny_z = [
        push(small_z.at[c, z], small_z.at[c, z], at(dz=d)) for d in (1, 3, 2)
    ]
    pass_far(0)
    pass_far(1)
    enter(1, 1, parts=(0, 1, 2))
    from_sibling(2)
    by_left(6, 2, False)
    by_left(6, 2, True)
    send_sums(0)
    relay(1)
    arrived(1, 1, 6)
    enter(1, 1, parts=(3,))
    enter(1, 2, 2, 4)
    times(0, 2, 1)
    relay_last_side(0)
    times(2, 2, 4)
    relay_last_side(1)
    for copy in tiny_z:
        copy.wait_recv()
    tiny_c = push(small_z.at[c], small_z.at[c], at(dc=1))
    arrived(3, 1, 6)
    arrived(7, 1, 6)
    for lanes in sides:
        arrived(7, 1, 0, lanes=lanes)
    enter(1, 3, 2, 4)
    times(3, 2, 4)
    arrived(5, 1, 6)
    enter(1, 4, 2, parts=(3,))
    for slot in (4, 5):
        arrived(slot, 1, 0, lanes=sides[0])
    enter(1, 4, 2, 1, (0, 1, 2), sides[0])
    times(4, 2, 1, (1,), sides[0])
    send_sums(1, sides[0])
    for slot in (4, 5):
        arrived(slot, 1, 0, lanes=sides[1])
    enter(1, 4, 2, 1, (0, 1), sides[1])
    for slot in (4, 5):
        arrived(slot, 1, 4, lanes=sides[1])
    enter(1, 4, 2, 1, (2,), sides[1])
    times(4, 2, 1, (1,), sides[1])
    send_sums(1, sides[1])
    times(4, 2, 1, (0,))
    tiny_c.wait_recv()

    rows_z = [(r // 2, r % 2) for r in range(8)]
    one = jnp.concatenate([small_z[cc, zz, 0:8, :] for zz, cc in rows_z], 0)
    coll = jnp.concatenate([small_z[cc, zz, 8:16, :] for zz, cc in rows_z], 0)
    gr, gi = one[:, 0:64], one[:, 64:128]
    cr, ci = coll[:, 0:64], coll[:, 64:128]
    density = jnp.sum(gr * eye, 0, keepdims=True)
    hartree_col = jnp.sum(coup[...] * density, 1, keepdims=True)
    diag_col = hartree_col + jnp.sum(hr * eye, 1, keepdims=True)
    diag_row = jnp.sum(diag_col * eye, 0, keepdims=True)
    fr = off_r + diag_col * eye
    fi = off_i
    comm_r = dot(fr, gr) - dot(fi, gi) - dot(gr, fr) + dot(gi, fi)
    comm_i = dot(fr, gi) + dot(fi, gr) - dot(gr, fi) - dot(gi, fr)
    d1_r[...] = comm_i + cr + cr.T
    d1_i[...] = ci - ci.T - comm_r

    from_cols = jnp.zeros((1, 256), F32)
    lane_group = iota((1, 256), 1) // 64
    row64 = iota((64, 64), 0)
    table = coup[...] + diag_col + diag_row
    table_wide = dot(table, repeat)
    row_wide = iota((64, 256), 0)
    for k in range(COLS):
        picked = jnp.sum(
            jnp.where(row_wide == cb * COLS + k, table_wide, 0.0), 0, keepdims=True
        )
        from_cols = jnp.where(lane_group == k, picked, from_cols)
    table_t = coup_t + diag_col + diag_row
    for i in range(ROWS):
        from_rows = jnp.sum(
            jnp.where(iota((64, 64), 1) == rb * ROWS + i, table_t, 0.0), 1, keepdims=True
        )
        rows = slice(i * 64, i * 64 + 64)
        factor = from_rows - from_cols
        out_r[rows, :] += factor * g2i[rows, :]
        out_i[rows, :] -= factor * g2r[rows, :]

    for ch in range(2):
        for g in range(2):
            sums[ch, g, 0].wait_recv()
            if ch == 1:
                sums[1, g, 128].wait_recv()
            lanes = slice(g * 128, g * 128 + 128)
            for comp in range(2):
                for ip in range(2):
                    cut = slice(ip * 128, ip * 128 + 128)
                    even, odd = half_swap(
                        part[ch, g, comp, 0:64, cut] + part_in[ch, g, comp, 0:64, cut],
                        part[ch, g, comp, 64:128, cut] + part_in[ch, g, comp, 64:128, cut],
                        lower,
                    )
                    top = ch * 256 + ip * 128
                    for first, value in ((top, even), (top + 64, odd)):
                        if comp == 0:
                            out_i[first : first + 64, lanes] -= value
                        else:
                            out_r[first : first + 64, lanes] += value
    for copy in sent:
        copy.wait_send()


def finish(a, b, c, d, out_a, out_b, out_c, out_d):
    for src, dst in ((a, out_a), (b, out_b), (c, out_c), (d, out_d)):
        dst[...] = src[...]


def on_device(g2_re, g2_im, g1_re, g1_im, hop_re, hop_im, coupling):
    vmem = pl.BlockSpec(memory_space=pltpu.VMEM)
    smem = pl.BlockSpec(memory_space=pltpu.SMEM)
    count = 96
    shapes = (
        jax.ShapeDtypeStruct((512, 256), F32),
        jax.ShapeDtypeStruct((512, 256), F32),
        jax.ShapeDtypeStruct((64, 64), F32),
        jax.ShapeDtypeStruct((64, 64), F32),
    )
    parts = pl.pallas_call(
        kernel,
        out_shape=shapes,
        in_specs=[vmem] * 7 + [smem] * 2,
        out_specs=(vmem,) * 4,
        scratch_shapes=[
            pltpu.VMEM((8, 2, 8, 64, 256), F32),
            pltpu.VMEM((8, 2, 2, 256, 256), F32),
            pltpu.VMEM((2, 2, 128, 256), F32),
            pltpu.VMEM((8, 2, 1536, 256), BF16),
            pltpu.VMEM((8, 512, 1024), BF16),
            pltpu.VMEM((2, 4, 2, 128, 256), F32),
            pltpu.VMEM((2, 2, 2, 128, 256), F32),
            pltpu.VMEM((4, 16, 128), F32),
            pltpu.VMEM((4, 16, 128), F32),
            pltpu.VMEM((2, 4, 16, 128), F32),
            pltpu.VMEM((2, 64, 512), F32),
            pltpu.VMEM((2, 256, 256), F32),
            pltpu.VMEM((64, 256), F32),
            pltpu.SemaphoreType.DMA((count,)),
            pltpu.SemaphoreType.DMA((count,)),
        ],
        compiler_params=pltpu.CompilerParams(
            collective_id=0, has_side_effects=True, vmem_limit_bytes=56 * 2**20
        ),
    )(g2_re, g2_im, g1_re.T, g1_im.T, hop_re, hop_im, coupling, hop_re, hop_im)
    return pl.pallas_call(
        finish, out_shape=shapes, in_specs=[vmem] * 4, out_specs=(vmem,) * 4
    )(*parts)


def solution(mesh):
    pairs = P("prow", ("pcol", "orb"))
    return jax.shard_map(
        on_device,
        mesh=mesh,
        in_specs=(pairs, pairs, pairs, pairs, P(), P(), P()),
        out_specs=(pairs, pairs, P(), P()),
        check_vma=False,
    )
```
